512 devices in a mesh: gx: 8 (over z), gy: 4 (over x), gz: 16 (over y, core).
Axes of the slice: x: 4, y: 8, z: 8, core: 2. Of those that a mesh axis runs over, the one named last changes fastest.
Arguments:
- log_perm: float32 [32, 64, 2048], P('gx', 'gy', 'gz'), may hold values from -1 to 1
- pressure: float32 [32, 64, 2048], P('gx', 'gy', 'gz'), may hold values from -4 to 4
- data_weight: float32 [32, 64, 2048], P('gx', 'gy', 'gz'), may hold values from 1 to 30
- probes: float32 [16, 32, 64, 2048], P(None, 'gx', 'gy', 'gz'), may hold values from -3 to 3
Outputs:
- basis: float32 [16, 32, 64, 2048], P(None, 'gx', 'gy', 'gz')
- factor: float32 [16, 16], replicated
The draws below stay inside these ranges and needn't reach their ends.
All inputs are finite; a program needn't handle non-finite values.
Results may differ from the reference program's by a relative error of at most 0.00029.
Values sent between devices are 32-bit elements; how exact they have to be, the bound alone decides.
No kernel may reach another device: no remote copies, remote signals or barrier semaphores. Data moves between devices by JAX's collectives and lax.ppermute only.
A program may use at most 64 MiB of HBM per device.

```python
import math
import jax
import jax.numpy as jnp
from jax import lax

PROBES = 16
DEG = 4
NX = 32
NY = 64
NZ = 2048


def draw_probes(key, part):
    key = jax.random.fold_in(key, 11)
    key_scale, key_noise = jax.random.split(key, 2)
    scales = jnp.exp(jax.random.uniform(key_scale, (PROBES, 1, 1, 1), jnp.float32, math.log(0.1), 0.0))
    noise = jax.random.normal(key_noise, (PROBES, NX, NY, NZ), jnp.float32)
    return jnp.clip(noise, -3.0, 3.0) * scales


def draw_data_weight(key, part):
    key = jax.random.fold_in(key, 23)
    level = jnp.exp(jax.random.uniform(key, (NX, NY, NZ), jnp.float32, 0.0, math.log(10.0)))
    trend = 1.0 + 2.0 * jnp.arange(NZ, dtype=jnp.float32) / max(NZ - 1, 1)
    return level * trend[None, None, :]


def level_of(rng, shape, pieces, smallest, top_value):
    def one(dim, parts):
        steps = jax.random.uniform(jax.random.fold_in(jax.random.fold_in(rng, 6), dim), (parts,), jnp.float32, smallest / len(pieces), top_value / len(pieces))
        return jnp.repeat(jnp.exp(steps), shape[dim] // parts).reshape((-1,) + (1,) * (len(shape) - dim - 1))

    level = one(*pieces[0])
    for cut in pieces[1:]:
        level = level * one(*cut)
    return level


def normal_values(key, extent, width, limit, cuts=(), kind=jnp.bfloat16):
    drawn = jax.random.normal(key, extent, jnp.float32) * width
    if len(cuts) > 0:
        drawn = level_of(key, extent, cuts, -0.22, 0.18) * drawn
    return jnp.clip(drawn, min=-limit, max=limit).astype(kind)


def setup_inputs(seed: int = 0) -> dict:
    key_of = jax.random.split(jax.random.key(seed), 5)
    return {
        "log_perm": jnp.clip(jax.random.uniform(key_of[0], (NX, NY, NZ), jnp.float32, -1.0, 1.0) * level_of(key_of[0], (NX, NY, NZ), ((0, 8), (1, 4), (2, 16)), -0.4, 0.0), -1.0, 1.0),
        "pressure": normal_values(key_of[1], (NX, NY, NZ), 1.0, 4.0, ((0, 8), (1, 4), (2, 16)), jnp.float32),
        "data_weight": draw_data_weight(jax.random.fold_in(key_of[4], 71), 0),
        "probes": draw_probes(jax.random.fold_in(key_of[4], 71), 0),
    }


reaction_shift = 0.5
lower_bound = 0.5
upper_bound = 33.5

def neighbours(padded):
    return [padded[..., 2:, 1:-1, 1:-1], padded[..., :-2, 1:-1, 1:-1], padded[..., 1:-1, 2:, 1:-1], padded[..., 1:-1, :-2, 1:-1], padded[..., 1:-1, 1:-1, 2:], padded[..., 1:-1, 1:-1, :-2]]

def middle(padded):
    return padded[..., 1:-1, 1:-1, 1:-1]

def operate_padded(field_pad, perm_pad):
    centre = middle(field_pad)
    perm_mid = middle(perm_pad)
    summed = reaction_shift * centre
    for field_nb, perm_nb in zip(neighbours(field_pad), neighbours(perm_pad)):
        summed = summed + 0.5 * (perm_mid + perm_nb) * (centre - field_nb)
    return summed

def forward_term(scaled_pad, press_pad):
    centre = middle(scaled_pad)
    press_mid = middle(press_pad)
    summed = jnp.zeros_like(centre)
    for scaled_nb, press_nb in zip(neighbours(scaled_pad), neighbours(press_pad)):
        summed = summed + 0.5 * (centre + scaled_nb) * (press_mid - press_nb)
    return summed

def adjoint_term(dual_pad, press_pad, permeability):
    centre = middle(dual_pad)
    press_mid = middle(press_pad)
    summed = jnp.zeros_like(centre)
    for dual_nb, press_nb in zip(neighbours(dual_pad), neighbours(press_pad)):
        summed = summed + (centre - dual_nb) * (press_mid - press_nb)
    return 0.5 * permeability * summed

def chebyshev(source, apply_op):
    mid_eig = (upper_bound + lower_bound) / 2.0
    half_width = (upper_bound - lower_bound) / 2.0
    ratio_sig = mid_eig / half_width
    weight_now = 1.0 / ratio_sig
    residual = source
    direction = source / mid_eig
    iterate = direction
    for repeat in range(DEG):
        residual = residual - apply_op(direction)
        weight_next = 1.0 / (2.0 * ratio_sig - weight_now)
        direction = weight_next * weight_now * direction + 2.0 * weight_next / half_width * residual
        iterate = iterate + direction
        weight_now = weight_next
    return iterate

def reference(log_perm, pressure, data_weight, probes):
    permeability = jnp.exp(log_perm)
    perm_pad = jnp.pad(permeability, 1)
    press_pad = jnp.pad(pressure, 1)

    def apply_op(field_in):
        return operate_padded(jnp.pad(field_in, 1), perm_pad)

    def one_probe(probe_row):
        source = forward_term(jnp.pad(permeability * probe_row, 1), press_pad)
        state_field = chebyshev(source, apply_op)
        dual_field = chebyshev(data_weight * state_field, apply_op)
        return adjoint_term(jnp.pad(dual_field, 1), press_pad, permeability)
    images = lax.map(one_probe, probes)
    flat_images = images.reshape(PROBES, -1)
    cell_count = NX * NY * NZ
    gram_matrix = jnp.dot(flat_images.astype(jnp.float32), flat_images.T.astype(jnp.float32), precision=lax.Precision.HIGHEST, preferred_element_type=jnp.float32) / cell_count
    lower_factor = jnp.linalg.cholesky(gram_matrix)
    basis_rows = lax.linalg.triangular_solve(lower_factor, flat_images, left_side=True, lower=True)
    return (basis_rows.reshape(probes.shape), lower_factor.T)
```

```python
import jax
import jax.numpy as jnp
from jax import lax
from jax.experimental import pallas as pl
from jax.experimental.pallas import tpu as pltpu
from jax.sharding import PartitionSpec as P

DEG = 4
SHIFT = 0.5
LOWER = 0.5
UPPER = 33.5
MID = (UPPER + LOWER) / 2.0
HALF = (UPPER - LOWER) / 2.0
RATIO = MID / HALF

PROBES = 16
CELLS = 32 * 64 * 2048
WIN = 16
HALO = 2 * DEG + 2
INNER = DEG + 1
ROWS = WIN + 2 * HALO
UNROLL = 4
MSG = 12 * HALO + 4 * INNER
F32 = jnp.float32


def lane_sub():
    lane = lax.broadcasted_iota(jnp.int32, (8, 128), 1)
    return lane, lax.broadcasted_iota(jnp.int32, (8, 128), 0)


def swap_groups(v):
    lane, _ = lane_sub()
    high, low = (lane & 64) == 0, (lane & 32) == 0
    u = [None] * 4
    for a in range(2):
        u[a] = jnp.where(high, v[a], pltpu.roll(v[a + 2], 64, 1))
        u[a + 2] = jnp.where(high, pltpu.roll(v[a], 64, 1), v[a + 2])
    out = [None] * 4
    for a in (0, 2):
        out[a] = jnp.where(low, u[a], pltpu.roll(u[a + 1], 32, 1))
        out[a + 1] = jnp.where(low, pltpu.roll(u[a], 96, 1), u[a + 1])
    return out


def x_up(v):
    return [pltpu.roll(v[n - 3], 7, 0) if n % 4 == 3 else v[n + 1] for n in range(8)]


def y_up(v):
    return [v[n + 4] if n < 4 else pltpu.roll(v[n - 4], 124, 1) for n in range(8)]


def pack_kernel(lp_ref, pr_ref, dw_ref, v_ref, out_ref, perm_ref, mix_ref):
    perm_ref[...] = jnp.exp(lp_ref[...])
    first = (lane_sub()[0] & 2) == 0

    def mixed(parts):
        for slot in range(4):
            mix_ref[pl.ds(slot, 32, stride=4), :] = parts[slot]
        return mix_ref[...].T

    def half(ref, yl):
        return ref[pl.ds(yl, 32, stride=2), :]

    def paired(tile, w):
        return jnp.where(first, tile[16 * w : 16 * w + 8], tile[16 * w + 8 : 16 * w + 16])

    for yl in range(2):
        perm = half(perm_ref, yl)
        for q in range(4):
            tile = mixed([perm * v_ref[4 * q + p, pl.ds(yl, 32, stride=2), :] for p in range(4)])
            for w in range(8):
                out_ref[4 * w + q, 16 * yl : 16 * yl + 16] = tile[16 * w : 16 * w + 16]
        tile = mixed([perm, half(pr_ref, yl)] * 2)
        for w in range(8):
            packed = paired(tile, w)
            for q in range(4):
                out_ref[4 * w + q, 32 + 8 * yl : 40 + 8 * yl] = packed
    tile = mixed([half(dw_ref, 0), half(dw_ref, 1)] * 2)
    for w in range(8):
        packed = paired(tile, w)
        for q in range(4):
            out_ref[4 * w + q, 48:56] = packed


def widen(v, first):
    return jnp.where(first, v, pltpu.roll(v, 2, 1)), jnp.where(first, pltpu.roll(v, 126, 1), v)


def split(v, even):
    return jnp.where(even, v, pltpu.roll(v, 1, 1)), jnp.where(even, pltpu.roll(v, 127, 1), v)


def arrange_kernel(in_ref, s_ref, c_ref, w_ref, low_ref, high_ref):
    lane, _ = lane_sub()
    first = (lane & 2) == 0

    def fetch(rows):
        got = [[in_ref[pl.ds(56 * g + row, 8, stride=224), :] for g in range(4)] for row in rows]
        return [swap_groups(v) for v in got]

    lift, pairs = WIN - HALO, HALO // 2
    for yl in range(2):
        for batch in range(0, WIN, 8):
            got = fetch([16 * yl + batch + k for k in range(8)])
            for k in range(8):
                z = batch + k
                for x, v in enumerate(got[k]):
                    n = 4 * yl + x
                    s_ref[z, n] = v
                    if z < HALO:
                        low_ref[8 * z + n] = v
                    if z >= lift:
                        high_ref[8 * (z - lift) + n] = v
        got = fetch([32 + 8 * yl + z for z in range(8)])
        for x in range(4):
            n = 4 * yl + x
            wide = [widen(got[z][x], first) for z in range(8)]
            c = [v[0] for v in wide] + [v[1] for v in wide]
            for z in range(WIN):
                c_ref[z, n] = c[z]
            for k in range(pairs):
                at = 8 * HALO + 8 * k + n
                low_ref[at] = jnp.where(first, c[k], c[k + pairs])
                high_ref[at] = jnp.where(first, c[lift + k], c[lift + k + pairs])
    got = fetch([48 + z for z in range(8)])
    wide = [[widen(v, first) for v in got[z]] for z in range(8)]
    for z in range(8):
        for x in range(4):
            below, above = wide[z][x]
            w_ref[z, x] = below
            w_ref[z + 8, x] = above
            if z < INNER:
                low_ref[12 * HALO + 4 * z + x] = below
            if z + 8 >= WIN - INNER:
                high_ref[12 * HALO + 4 * (z + 8 - WIN + INNER) + x] = above


def core_kernel(
    edge_ref, lo_ref, s_own_ref, c_own_ref, w_own_ref, hi_ref, out_ref,
    kx_ref, ky_ref, kz_ref, kd_ref, diag_ref, dx_ref, dy_ref, dz_ref, dd_ref, pd_ref,
    perm_ref, press_ref, wt_ref, s_ref, r_ref, e0_ref, e1_ref, z_ref,
):
    lane, sub = lane_sub()
    first, even = (lane & 2) == 0, (lane & 1) == 0
    at_first, at_last = edge_ref[0], edge_ref[1]

    def fill(k, base, inner, s, c, w, count):
        c = [split(v, even) for v in c]
        w = [split(v, even) for v in w]
        for n in range(8 * count):
            if s:
                s_ref[base + n // 8, n % 8] = s[n]
        for n in range(len(c)):
            perm_ref[base + n // 8, n % 8], press_ref[base + n // 8, n % 8] = c[n]
        for n in range(len(w)):
            row, x = inner + n // 4, n % 4
            wt_ref[row, x], wt_ref[row, 4 + x] = w[n]

    def fill_own(i, carry):
        k = 2 * i
        s = [s_own_ref[k + n // 8, n % 8] for n in range(16)]
        c = [c_own_ref[k + n // 8, n % 8] for n in range(16)]
        w = [w_own_ref[k + n // 4, n % 4] for n in range(8)]
        fill(k, HALO + k, INNER + k, s, c, w, 2)
        return carry

    lax.fori_loop(0, WIN // 2, fill_own, 0)
    pairs = HALO // 2
    for src_ref, base, inner in ((lo_ref, 0, 0), (hi_ref, HALO + WIN, INNER + WIN)):
        for k in range(HALO):
            for n in range(8):
                s_ref[base + k, n] = src_ref[8 * k + n]
        wide = [widen(src_ref[8 * HALO + i], first) for i in range(8 * pairs)]
        w = [src_ref[12 * HALO + i] for i in range(4 * INNER)]
        fill(0, base, inner, [], [v[0] for v in wide], w, 0)
        fill(0, base + pairs, inner, [], [v[1] for v in wide], [], 0)

    def mark(n):
        none = jnp.zeros((8, 128), F32)
        return (
            jnp.where(sub == 0, 0.5, 0.0) if n % 4 == 0 else none,
            jnp.where(sub == 7, 0.5, 0.0) if n % 4 == 3 else none,
            jnp.where(lane < 4, 0.5, 0.0) if n < 4 else none,
            jnp.where(lane >= 124, 0.5, 0.0) if n >= 4 else none,
        )

    ends = [mark(n) for n in range(8)]

    def coefficients(row, carry):
        here, above = jnp.int32(row == HALO), jnp.int32(row == HALO + WIN - 1)
        below = jnp.int32(row == HALO - 1)
        out_z = 0.5 * (here * at_first + above * at_last).astype(F32)
        half_z = 0.5 * (1 - below * at_first - above * at_last).astype(F32)
        perm = [perm_ref[row, n] for n in range(8)]
        press = [press_ref[row, n] for n in range(8)]
        perm_z = [perm_ref[row + 1, n] for n in range(8)]
        press_z = [press_ref[row + 1, n] for n in range(8)]
        perm_x, perm_y, press_x, press_y = x_up(perm), y_up(perm), x_up(press), y_up(press)
        outs = []
        for n in range(8):
            x_begin, x_end, y_begin, y_end = ends[n]
            outside = (x_begin + x_end) + (y_begin + y_end) + out_z
            half_x, half_y = 0.5 - x_end, 0.5 - y_end
            outs.append((kx_ref, n, half_x * (perm[n] + perm_x[n])))
            outs.append((ky_ref, n, half_y * (perm[n] + perm_y[n])))
            outs.append((kz_ref, n, half_z * (perm[n] + perm_z[n])))
            outs.append((diag_ref, n, SHIFT + outside * perm[n]))
            outs.append((dx_ref, n, half_x * (press[n] - press_x[n])))
            outs.append((dy_ref, n, half_y * (press[n] - press_y[n])))
            outs.append((dz_ref, n, half_z * (press[n] - press_z[n])))
            outs.append((pd_ref, n, outside * press[n]))
        lower = x_far(perm, press) + y_far(perm, press)
        for i, n in enumerate((0, 4, 0, 1, 2, 3)):
            half = 0.5 - ends[n][0 if i < 2 else 2]
            outs.append((kd_ref, i, half * (perm[n] + lower[i][0])))
            outs.append((dd_ref, i, half * (lower[i][1] - press[n])))
        for ref, n, value in outs:
            ref[row, n] = value
        return carry

    def x_far(a, b):
        return [(pltpu.roll(a[n + 3], 1, 0), pltpu.roll(b[n + 3], 1, 0)) for n in (0, 4)]

    def y_far(a, b):
        return [(pltpu.roll(a[n + 4], 4, 1), pltpu.roll(b[n + 4], 4, 1)) for n in range(4)]

    lax.fori_loop(0, ROWS - 1, coefficients, 0)

    def load(ref, row, count=8):
        return [ref[row, n] for n in range(count)]

    def far(v):
        return (
            [pltpu.roll(v[n], 7, 0) for n in (0, 4)]
            + [pltpu.roll(v[n], 1, 0) for n in (3, 7)]
            + [pltpu.roll(v[n], 124, 1) for n in range(4)]
            + [pltpu.roll(v[n + 4], 4, 1) for n in range(4)]
        )

    def sweep(field_ref, begin, end, face_refs, centre_ref, join, sign, inputs, finish):
        fx_ref, fy_ref, fz_ref, fd_ref = face_refs

        def part(up, down):
            return up - down if sign < 0 else up + down

        def rows(row, count, carry):
            now, around, before = carry
            results = []
            for u in range(count):
                later = load(field_ref, row + u + 1)
                later_around = far(later)
                fx, fy, fz = (load(ref, row + u) for ref in (fx_ref, fy_ref, fz_ref))
                fd, centre = load(fd_ref, row + u, 6), load(centre_ref, row + u)
                flow_x, back_x, flow_y, back_y = ([None] * 8 for _ in range(4))
                for n in range(8):
                    up = now[n + 1] if n % 4 < 3 else around[n // 4]
                    flow_x[n] = join(now[n], up) * fx[n]
                    up = now[n + 4] if n < 4 else around[n]
                    flow_y[n] = join(now[n], up) * fy[n]
                for n in range(8):
                    if n % 4:
                        back_x[n] = flow_x[n - 1]
                    else:
                        back_x[n] = join(around[2 + n // 4], now[n]) * fd[n // 4]
                    if n >= 4:
                        back_y[n] = flow_y[n - 4]
                    else:
                        back_y[n] = join(around[8 + n], now[n]) * fd[2 + n]
                flow_z = [join(now[n], later[n]) * fz[n] for n in range(8)]
                for n in range(8):
                    total = centre[n] * now[n] + part(flow_x[n], back_x[n])
                    total = total + (part(flow_y[n], back_y[n]) + part(flow_z[n], before[n]))
                    extra = [ref[row + u, n] for ref in inputs]
                    results.append((row + u, n, finish(row + u, n, now[n], total, *extra)))
                now, around, before = later, later_around, flow_z
            for at, n, outs in results:
                for put, value in outs:
                    put(at, n, value)
            return now, around, before

        now, later = load(field_ref, begin - 1), load(field_ref, begin)
        fz = load(fz_ref, begin - 1)
        carry = later, far(later), [join(now[n], later[n]) * fz[n] for n in range(8)]
        steps, rest = divmod(end - begin, UNROLL)
        carry = lax.fori_loop(
            0, steps, lambda i, c: rows(begin + UNROLL * i, UNROLL, c), carry
        )
        if rest:
            rows(end - rest, rest, carry)

    def add(a, b):
        return a + b

    def minus(a, b):
        return a - b

    def into(ref):
        def put(row, n, value):
            ref[row, n] = value

        return put

    def start(value):
        direction = value * (1.0 / MID)
        return [(into(r_ref), value), (into(e0_ref), direction), (into(z_ref), direction)]

    def solve(lowest, finish_last):
        weight_now = 1.0 / RATIO
        here, there = e0_ref, e1_ref
        for repeat in range(DEG):
            weight_next = 1.0 / (2.0 * RATIO - weight_now)
            keep, take = weight_next * weight_now, 2.0 * weight_next / HALF
            weight_now = weight_next
            last = repeat == DEG - 1

            def finish(row, n, v, total, residual, iterate, k=keep, m=take, to=there, last=last):
                residual = residual - total
                direction = k * v + m * residual
                iterate = iterate + direction
                if last:
                    return finish_last(row, n, iterate)
                return [(into(r_ref), residual), (into(to), direction), (into(z_ref), iterate)]

            begin = lowest + 1 + repeat
            faces = (kx_ref, ky_ref, kz_ref, kd_ref)
            sweep(here, begin, ROWS - begin, faces, diag_ref, minus, -1, (r_ref, z_ref), finish)
            here, there = there, here

    faces = (dx_ref, dy_ref, dz_ref, dd_ref)
    sweep(
        s_ref, 1, ROWS - 1, faces, pd_ref, add, -1, (), lambda row, n, v, total: start(total)
    )
    skip = HALO - INNER
    solve(1, lambda row, n, value: start(value * wt_ref[row - skip, n]))
    solve(skip, lambda row, n, value: [(into(s_ref), value)])

    def image(row, n, v, total):
        return [(into(z_ref), perm_ref[row, n] * total)]

    sweep(s_ref, HALO, HALO + WIN, faces, pd_ref, minus, 1, (), image)

    def send(i, carry):
        got = [
            (4 * i + k, yl, [z_ref[HALO + 4 * i + k, 4 * yl + x] for x in range(4)])
            for k in range(4)
            for yl in range(2)
        ]
        for k, yl, v in [(k, yl, swap_groups(v)) for k, yl, v in got]:
            for g in range(4):
                out_ref[pl.ds(g * 2 * WIN + yl * WIN + k, 8, stride=8 * WIN), :] = v[g]
        return carry

    lax.fori_loop(0, WIN // 4, send, 0)


def gram_kernel(in_ref, img_ref, gram_ref, acc_ref, mix_ref):
    for q in range(4):
        for yl in range(2):
            rows = [in_ref[4 * w + q, 16 * yl : 16 * yl + 16] for w in range(8)]
            mix_ref[...] = jnp.concatenate(rows, axis=0).T
            for p in range(4):
                img_ref[4 * q + p, pl.ds(yl, 32, stride=2), :] = mix_ref[pl.ds(p, 32, stride=4), :]
    for i in range(PROBES):
        a = [img_ref[i, 8 * k : 8 * k + 8] for k in range(8)]
        for j in range(i + 1):
            parts = [a[k] * img_ref[j, 8 * k : 8 * k + 8] for k in range(8)]
            while len(parts) > 1:
                parts = [parts[k] + parts[k + 1] for k in range(0, len(parts), 2)]
            begin = (16 * i + j) * 8
            acc_ref[begin : begin + 8] = parts[0]
            begin = (16 * j + i) * 8
            acc_ref[begin : begin + 8] = parts[0]
    sums = []
    for c in range(32):
        parts = [acc_ref[pl.ds(64 * c + s, 8, stride=8), :] for s in range(8)]
        while len(parts) > 1:
            parts = [parts[k] + parts[k + 1] for k in range(0, len(parts), 2)]
        sums.append(parts[0])
    total = lax.dot_general(
        jnp.ones((8, 128), F32),
        jnp.concatenate(sums, axis=0),
        (((1,), (1,)), ((), ())),
        precision=lax.Precision.HIGHEST,
        preferred_element_type=F32,
    )
    _, sub = lane_sub()
    tile = jnp.where(sub == 0, total[:, :128], total[:, 128:])
    for d in range(32):
        gram_ref[d] = tile


def spread_kernel(in_ref, out_ref):
    total = jnp.sum(in_ref[...], axis=0)
    for d in range(16):
        out_ref[d] = total


def finish_kernel(gram_ref, img_ref, out_ref, factor_ref, inv_ref):
    total = jnp.sum(gram_ref[...], axis=0) * (1.0 / CELLS)
    lane = lax.broadcasted_iota(jnp.int32, (16, 128), 1)
    row = lax.broadcasted_iota(jnp.int32, (16, 128), 0)
    g = jnp.concatenate(
        [jnp.broadcast_to(total[0:1], (8, 128)), jnp.broadcast_to(total[1:2], (8, 128))], axis=0
    )
    g = jnp.where((lane >> 4) == (row & 7), g, 0.0)
    for step in (16, 32, 64):
        g = g + pltpu.roll(g, step, 1)
    g = jnp.where(lane < 16, g, jnp.where(lane == row + 16, 1.0, 0.0))
    for k in range(PROBES - 1):
        pivot_row = jnp.broadcast_to(g[k : k + 1], (16, 128))
        column = jnp.broadcast_to(g[:, k : k + 1], (16, 128))
        pivot = jnp.broadcast_to(pivot_row[:, k : k + 1], (16, 128))
        g = g - jnp.where(row > k, column / pivot, 0.0) * pivot_row
    diagonal = jnp.sum(jnp.where(lane == row, g, 0.0), axis=1, keepdims=True)
    g = g / jnp.sqrt(diagonal)
    factor_ref[...] = jnp.where(lane >= row, g, 0.0)[:, :16]
    for j in range(PROBES):
        inv_ref[j] = jnp.broadcast_to(g[:, 16 + j : 17 + j], (16, 128))
    for i in range(PROBES):
        scale = [jnp.broadcast_to(inv_ref[j, i : i + 1], (8, 128)) for j in range(i + 1)]
        for k in range(8):
            value = scale[0] * img_ref[0, 8 * k : 8 * k + 8]
            for j in range(1, i + 1):
                value = value + scale[j] * img_ref[j, 8 * k : 8 * k + 8]
            out_ref[i, 8 * k : 8 * k + 8] = value


def call(kernel, out_shapes, scratch=(), smem=0, inputs=1):
    out_shape = [jax.ShapeDtypeStruct(s, F32) for s in out_shapes]
    vmem = pl.BlockSpec(memory_space=pltpu.VMEM)
    specs = [pl.BlockSpec(memory_space=pltpu.SMEM)] * smem + [vmem] * inputs
    return pl.pallas_call(
        kernel,
        out_shape=out_shape,
        in_specs=specs,
        out_specs=[vmem] * len(out_shape),
        scratch_shapes=[pltpu.VMEM(s, F32) for s in scratch],
        compiler_params=pltpu.CompilerParams(vmem_limit_bytes=40 * 1024 * 1024),
    )


def on_device(log_perm, pressure, data_weight, probes):
    planes = [a.reshape(64, 128) for a in (log_perm, pressure, data_weight)]
    (sent,) = call(pack_kernel, [(32, 56, 128)], [(64, 128), (128, 128)], inputs=4)(
        *planes, probes.reshape(16, 64, 128)
    )
    got = lax.all_to_all(sent, ("gx", "gy"), 0, 0)
    plane, msg = (WIN, 8, 8, 128), (MSG, 8, 128)
    own_s, own_c, own_w, low, high = call(
        arrange_kernel, [plane, plane, (WIN, 4, 8, 128), msg, msg]
    )(got.reshape(32 * 56, 128))

    size_x, size_z = lax.axis_size("gx"), lax.axis_size("gz")

    def place(n):
        return (n % size_x) * size_z + n // size_x

    count = size_x * size_z
    up = [(place(n), place(n + 1)) for n in range(count - 1)]
    down = [(j, i) for i, j in up]
    from_below = lax.ppermute(high, ("gx", "gz"), up)
    from_above = lax.ppermute(low, ("gx", "gz"), down)
    number = lax.axis_index("gz") * size_x + lax.axis_index("gx")
    edge = jnp.stack([number == 0, number == count - 1]).astype(jnp.int32)
    field = (ROWS, 8, 8, 128)
    far = (ROWS, 6, 8, 128)
    scratch = ([field] * 3 + [far, field]) * 2
    scratch += [field] * 2 + [(WIN + 2 * INNER, 8, 8, 128)] + [field] * 5
    (images,) = call(core_kernel, [(1024, 128)], scratch, smem=1, inputs=5)(
        edge, from_below, own_s, own_c, own_w, from_above
    )
    back = lax.all_to_all(images.reshape(32, 32, 128), ("gx", "gy"), 0, 0)
    image_rows, gram = call(gram_kernel, [(16, 64, 128), (32, 8, 128)], [(2048, 128), (128, 128)])(back)
    gram = lax.all_to_all(gram, ("gx", "gy"), 0, 0)
    (gram,) = call(spread_kernel, [(16, 8, 128)])(gram)
    gram = lax.all_to_all(gram, "gz", 0, 0)
    basis, factor = call(
        finish_kernel, [(16, 64, 128), (16, 16)], [(16, 16, 128)], inputs=2
    )(gram, image_rows)
    return (basis.reshape(probes.shape), factor)


def solution(mesh):
    in_specs = (
        P("gx", "gy", "gz"),
        P("gx", "gy", "gz"),
        P("gx", "gy", "gz"),
        P(None, "gx", "gy", "gz"),
    )
    out_specs = (P(None, "gx", "gy", "gz"), P())
    return jax.shard_map(
        on_device, mesh=mesh, in_specs=in_specs, out_specs=out_specs, check_vma=False
    )
```

```python
import jax
import jax.numpy as jnp
from jax import lax
from jax.experimental import pallas as pl
from jax.experimental.pallas import tpu as pltpu
from jax.sharding import PartitionSpec as P

DEG = 4
SHIFT = 0.5
LOWER = 0.5
UPPER = 33.5
MID = (UPPER + LOWER) / 2.0
HALF = (UPPER - LOWER) / 2.0
RATIO = MID / HALF

PROBES = 16
CELLS = 32 * 64 * 2048
WIN = 16
HALO = 2 * DEG + 2
INNER = DEG + 1
ROWS = WIN + 2 * HALO
UNROLL = 8
MSG = 12 * HALO + 4 * INNER
F32 = jnp.float32

PATHS = (
    ((0, 0), (0, 1), (1, 1), (1, 2), (0, 2), (0, 3), (1, 3), (1, 0)),
    ((1, 0), (1, 1), (2, 1), (2, 2), (1, 2), (1, 3), (2, 3), (2, 0)),
)


def place(block, w, q):
    core, layer = block % 2, block // 2
    gx = (PATHS[core][w][0] + 2 * (q + layer)) % 8
    return gx, PATHS[core][w][1]


def placer():
    block = lax.axis_index("gz")
    core, layer = block % 2, block // 2

    def number(w, q):
        (x0, y0), (x1, y1) = PATHS[0][w], PATHS[1][w]
        gx = (x0 + core * (x1 - x0) + 2 * (q + layer)) % 8
        return gx * 4 + y0 + core * (y1 - y0)

    return number


def lane_sub():
    lane = lax.broadcasted_iota(jnp.int32, (8, 128), 1)
    return lane, lax.broadcasted_iota(jnp.int32, (8, 128), 0)


def swap_groups(v):
    last = v[0].ndim - 1
    lane = lax.broadcasted_iota(jnp.int32, v[0].shape, last)
    high, low = (lane & 64) == 0, (lane & 32) == 0
    u = [None] * 4
    for a in range(2):
        moved = pltpu.roll(jnp.where(high, v[a + 2], v[a]), 64, last)
        u[a] = jnp.where(high, v[a], moved)
        u[a + 2] = jnp.where(high, moved, v[a + 2])
    out = [None] * 4
    for a in (0, 2):
        out[a] = jnp.where(low, u[a], pltpu.roll(u[a + 1], 32, last))
        out[a + 1] = jnp.where(low, pltpu.roll(u[a], 96, last), u[a + 1])
    return out


def pack_kernel(lp_hbm, pr_hbm, dw_hbm, v_hbm, out_ref, lp_ref, pr_ref, dw_ref, v_ref, perm_ref, mix_ref, sems):
    pairs = ((lp_hbm, lp_ref), (v_hbm, v_ref), (pr_hbm, pr_ref), (dw_hbm, dw_ref))
    copies = [pltpu.make_async_copy(a, b, sems.at[i]) for i, (a, b) in enumerate(pairs)]
    for copy in copies:
        copy.start()
    for copy in copies:
        copy.wait()
    perm_ref[...] = jnp.exp(lp_ref[...])
    first = (lane_sub()[0] & 2) == 0
    number = placer()
    dest = [[number(w, q) for q in range(4)] for w in range(8)]

    def mixed(parts):
        for slot in range(4):
            mix_ref[pl.ds(slot, 32, stride=4), :] = parts[slot]
        return mix_ref[...].T

    def half(ref, yl):
        return ref[pl.ds(yl, 32, stride=2), :]

    def paired(tile, w):
        return jnp.where(first, tile[16 * w : 16 * w + 8], tile[16 * w + 8 : 16 * w + 16])

    for yl in range(2):
        perm = half(perm_ref, yl)
        for q in range(4):
            tile = mixed([perm * v_ref[4 * q + p, pl.ds(yl, 32, stride=2), :] for p in range(4)])
            for w in range(8):
                out_ref[dest[w][q], 16 * yl : 16 * yl + 16] = tile[16 * w : 16 * w + 16]
        tile = mixed([perm, half(pr_ref, yl)] * 2)
        for w in range(8):
            packed = paired(tile, w)
            for q in range(4):
                out_ref[dest[w][q], 32 + 8 * yl : 40 + 8 * yl] = packed
    tile = mixed([half(dw_ref, 0), half(dw_ref, 1)] * 2)
    for w in range(8):
        packed = paired(tile, w)
        for q in range(4):
            out_ref[dest[w][q], 48:56] = packed


def widen(v, first):
    last = v.ndim - 1
    return jnp.where(first, v, pltpu.roll(v, 2, last)), jnp.where(first, pltpu.roll(v, 126, last), v)


def split(v, even):
    last = v.ndim - 1
    return jnp.where(even, v, pltpu.roll(v, 1, last)), jnp.where(even, pltpu.roll(v, 127, last), v)


def arrange_kernel(in_ref, s_ref, c_ref, w_ref, low_ref, high_ref):
    first = (lane_sub()[0] & 2) == 0

    def fetch(begin, count):
        got = [
            jnp.stack([in_ref[pl.ds(56 * g + begin + k, 8, stride=224), :] for k in range(count)])
            for g in range(4)
        ]
        return swap_groups(got)

    lift, pairs = WIN - HALO, HALO // 2
    for yl in range(2):
        for begin in range(0, WIN, 8):
            for x, v in enumerate(fetch(16 * yl + begin, 8)):
                n = 4 * yl + x
                s_ref[n, begin : begin + 8] = v
                for k in range(8):
                    z = begin + k
                    if z < HALO:
                        low_ref[HALO * n + z] = v[k]
                    if z >= lift:
                        high_ref[HALO * n + z - lift] = v[k]
        for x, v in enumerate(fetch(32 + 8 * yl, 8)):
            n = 4 * yl + x
            below, above = widen(v, first)
            c_ref[n, 0:8] = below
            c_ref[n, 8:16] = above
            c = [below[z] if z < 8 else above[z - 8] for z in range(WIN)]
            for k in range(pairs):
                at = 8 * HALO + pairs * n + k
                low_ref[at] = jnp.where(first, c[k], c[k + pairs])
                high_ref[at] = jnp.where(first, c[lift + k], c[lift + k + pairs])
    for x, v in enumerate(fetch(48, 8)):
        below, above = widen(v, first)
        w_ref[x, 0:8] = below
        w_ref[x, 8:16] = above
        at = 12 * HALO + INNER * x
        low_ref[at : at + INNER] = below[:INNER]
        high_ref[at : at + INNER] = above[8 - INNER :]


def core_kernel(
    edge_ref, lo_ref, s_own_ref, c_own_ref, w_own_ref, hi_ref, out_ref,
    kx_ref, ky_ref, kz_ref, kd_ref, diag_ref, dx_ref, dy_ref, dz_ref, dd_ref, pd_ref,
    perm_ref, press_ref, wt_ref, s_ref, r_ref, e0_ref, e1_ref, z_ref,
):
    lane, sub = lane_sub()
    first, even = (lane & 2) == 0, (lane & 1) == 0
    at_first, at_last = edge_ref[0].astype(F32), edge_ref[1].astype(F32)

    for n in range(8):
        s_ref[n, HALO : HALO + WIN] = s_own_ref[n]
        perm, press = split(c_own_ref[n], even)
        perm_ref[n, HALO : HALO + WIN] = perm
        press_ref[n, HALO : HALO + WIN] = press
    for x in range(4):
        low, high = split(w_own_ref[x], even)
        wt_ref[x, INNER : INNER + WIN] = low
        wt_ref[4 + x, INNER : INNER + WIN] = high
    pairs = HALO // 2
    for src_ref, base, inner in ((lo_ref, 0, 0), (hi_ref, HALO + WIN, INNER + WIN)):
        for n in range(8):
            begin = HALO * n
            s_ref[n, base : base + HALO] = src_ref[begin : begin + HALO]
            begin = 8 * HALO + pairs * n
            for part, c in enumerate(widen(src_ref[begin : begin + pairs], first)):
                at = base + pairs * part
                perm, press = split(c, even)
                perm_ref[n, at : at + pairs] = perm
                press_ref[n, at : at + pairs] = press
        for x in range(4):
            begin = 12 * HALO + INNER * x
            low, high = split(src_ref[begin : begin + INNER], even)
            wt_ref[x, inner : inner + INNER] = low
            wt_ref[4 + x, inner : inner + INNER] = high

    def mark(n):
        none = jnp.zeros((8, 128), F32)
        return (
            jnp.where(sub == 0, 0.5, 0.0) if n % 4 == 0 else none,
            jnp.where(sub == 7, 0.5, 0.0) if n % 4 == 3 else none,
            jnp.where(lane < 4, 0.5, 0.0) if n < 4 else none,
            jnp.where(lane >= 124, 0.5, 0.0) if n >= 4 else none,
        )

    ends = [mark(n) for n in range(8)]

    def far(v):
        return (
            [pltpu.roll(v[n], 7, 1) for n in (0, 4)]
            + [pltpu.roll(v[n], 1, 1) for n in (3, 7)]
            + [pltpu.roll(v[n], 124, 2) for n in range(4)]
            + [pltpu.roll(v[n + 4], 4, 2) for n in range(4)]
        )

    def coefficients(step, carry):
        here, above = pl.ds(5 * step, 5), pl.ds(5 * step + 1, 5)
        perm = [perm_ref[n, here] for n in range(8)]
        press = [press_ref[n, here] for n in range(8)]
        perm_far, press_far = far(perm), far(press)
        outs = []
        for n in range(8):
            x_begin, x_end, y_begin, y_end = ends[n]
            outside = (x_begin + x_end) + (y_begin + y_end)
            half_x, half_y = 0.5 - x_end, 0.5 - y_end
            near = (n + 1, None) if n % 4 < 3 else (None, n // 4)
            for field, field_far, out_ref, sign in (
                (perm, perm_far, kx_ref, 1.0),
                (press, press_far, dx_ref, -1.0),
            ):
                up = field_far[near[1]] if near[0] is None else field[near[0]]
                outs.append((out_ref, n, half_x * (field[n] + sign * up)))
            for field, field_far, out_ref, sign in (
                (perm, perm_far, ky_ref, 1.0),
                (press, press_far, dy_ref, -1.0),
            ):
                up = field[n + 4] if n < 4 else field_far[n]
                outs.append((out_ref, n, half_y * (field[n] + sign * up)))
            outs.append((kz_ref, n, 0.5 * (perm[n] + perm_ref[n, above])))
            outs.append((dz_ref, n, 0.5 * (press[n] - press_ref[n, above])))
            outs.append((diag_ref, n, SHIFT + outside * perm[n]))
            outs.append((pd_ref, n, outside * press[n]))
        for i, n in enumerate((0, 4, 0, 1, 2, 3)):
            half = 0.5 - ends[n][0 if i < 2 else 2]
            at = 2 + i if i < 2 else 6 + i
            outs.append((kd_ref, i, half * (perm[n] + perm_far[at])))
            outs.append((dd_ref, i, half * (press_far[at] - press[n])))
        for ref, n, value in outs:
            ref[n, here] = value
        return carry

    lax.fori_loop(0, (ROWS - 1) // 5, coefficients, 0)
    for row, inside, end in ((HALO - 1, HALO, at_first), (HALO + WIN - 1, HALO + WIN - 1, at_last)):
        for n in range(8):
            kz_ref[n, row] = kz_ref[n, row] * (1.0 - end)
            dz_ref[n, row] = dz_ref[n, row] * (1.0 - end)
            diag_ref[n, inside] = diag_ref[n, inside] + (0.5 * end) * perm_ref[n, inside]
            pd_ref[n, inside] = pd_ref[n, inside] + (0.5 * end) * press_ref[n, inside]

    def sweep(field_ref, begin, end, face_refs, centre_ref, join, sign, inputs, finish):
        fx_ref, fy_ref, fz_ref, fd_ref = face_refs

        def part(up, down):
            return up - down if sign < 0 else up + down

        def rows(row, count):
            here, below = pl.ds(row, count), pl.ds(row - 1, count + 1)
            now = [field_ref[n, here] for n in range(8)]
            around = far(now)
            flow_x, back_x, flow_y, back_y = ([None] * 8 for _ in range(4))
            for n in range(8):
                up = now[n + 1] if n % 4 < 3 else around[n // 4]
                flow_x[n] = join(now[n], up) * fx_ref[n, here]
                up = now[n + 4] if n < 4 else around[n]
                flow_y[n] = join(now[n], up) * fy_ref[n, here]
            for n in range(8):
                if n % 4:
                    back_x[n] = flow_x[n - 1]
                else:
                    back_x[n] = join(around[2 + n // 4], now[n]) * fd_ref[n // 4, here]
                if n >= 4:
                    back_y[n] = flow_y[n - 4]
                else:
                    back_y[n] = join(around[8 + n], now[n]) * fd_ref[2 + n, here]
            results = []
            for n in range(8):
                flow_z = join(field_ref[n, below], field_ref[n, pl.ds(row, count + 1)])
                flow_z = flow_z * fz_ref[n, below]
                total = centre_ref[n, here] * now[n] + part(flow_x[n], back_x[n])
                total = total + (part(flow_y[n], back_y[n]) + part(flow_z[1:], flow_z[:-1]))
                extra = [ref[n, here] for ref in inputs]
                results.append((n, finish(row, count, n, now[n], total, *extra)))
            for n, outs in results:
                for ref, value in outs:
                    ref[n, here] = value

        steps, rest = divmod(end - begin, UNROLL)

        def body(i, carry):
            rows(begin + UNROLL * i, UNROLL)
            return carry

        lax.fori_loop(0, steps, body, 0)
        if rest:
            rows(end - rest, rest)

    def add(a, b):
        return a + b

    def minus(a, b):
        return a - b

    def start(value):
        direction = value * (1.0 / MID)
        return [(r_ref, value), (e0_ref, direction), (z_ref, direction)]

    def solve(lowest, finish_last):
        weight_now = 1.0 / RATIO
        here, there = e0_ref, e1_ref
        for repeat in range(DEG):
            weight_next = 1.0 / (2.0 * RATIO - weight_now)
            keep, take = weight_next * weight_now, 2.0 * weight_next / HALF
            weight_now = weight_next
            last = repeat == DEG - 1

            def finish(row, count, n, v, total, residual, iterate, k=keep, m=take, to=there, last=last):
                residual = residual - total
                direction = k * v + m * residual
                iterate = iterate + direction
                if last:
                    return finish_last(row, count, n, iterate)
                return [(r_ref, residual), (to, direction), (z_ref, iterate)]

            begin = lowest + 1 + repeat
            faces = (kx_ref, ky_ref, kz_ref, kd_ref)
            sweep(here, begin, ROWS - begin, faces, diag_ref, minus, -1, (r_ref, z_ref), finish)
            here, there = there, here

    faces = (dx_ref, dy_ref, dz_ref, dd_ref)
    sweep(
        s_ref, 1, ROWS - 1, faces, pd_ref, add, -1, (), lambda row, count, n, v, total: start(total)
    )
    skip = HALO - INNER

    def second(row, count, n, value):
        return start(value * wt_ref[n, pl.ds(row - skip, count)])

    solve(1, second)
    solve(skip, lambda row, count, n, value: [(s_ref, value)])

    def image(row, count, n, v, total):
        return [(z_ref, perm_ref[n, pl.ds(row, count)] * total)]

    sweep(s_ref, HALO, HALO + WIN, faces, pd_ref, minus, 1, (), image)

    for yl in range(2):
        for begin in range(0, WIN, 8):
            at = slice(HALO + begin, HALO + begin + 8)
            v = swap_groups([z_ref[4 * yl + x, at] for x in range(4)])
            for g in range(4):
                for k in range(8):
                    to = g * 2 * WIN + yl * WIN + begin + k
                    out_ref[pl.ds(to, 8, stride=8 * WIN), :] = v[g][k]


def gram_kernel(in_ref, img_ref, gram_ref, acc_ref, mix_ref):
    number = placer()
    for q in range(4):
        source = [number(w, q) for w in range(8)]
        for yl in range(2):
            rows = [in_ref[source[w], 16 * yl : 16 * yl + 16] for w in range(8)]
            mix_ref[yl] = jnp.concatenate(rows, axis=0).T
            for p in range(4):
                img_ref[4 * q + p, pl.ds(yl, 32, stride=2), :] = mix_ref[
                    yl, pl.ds(p, 32, stride=4), :
                ]
    for i in range(PROBES):
        a = [img_ref[i, 8 * k : 8 * k + 8] for k in range(8)]
        for j in range(i + 1):
            parts = [a[k] * img_ref[j, 8 * k : 8 * k + 8] for k in range(8)]
            while len(parts) > 1:
                parts = [parts[k] + parts[k + 1] for k in range(0, len(parts), 2)]
            begin = (16 * i + j) * 8
            acc_ref[begin : begin + 8] = parts[0]
            begin = (16 * j + i) * 8
            acc_ref[begin : begin + 8] = parts[0]
    sums = []
    for c in range(32):
        parts = [acc_ref[pl.ds(64 * c + s, 8, stride=8), :] for s in range(8)]
        while len(parts) > 1:
            parts = [parts[k] + parts[k + 1] for k in range(0, len(parts), 2)]
        sums.append(parts[0])
    total = lax.dot_general(
        jnp.ones((8, 128), F32),
        jnp.concatenate(sums, axis=0),
        (((1,), (1,)), ((), ())),
        precision=lax.Precision.HIGHEST,
        preferred_element_type=F32,
    )
    _, sub = lane_sub()
    tile = jnp.where(sub == 0, total[:, :128], total[:, 128:])
    for d in range(32):
        gram_ref[d] = tile[0:2]


def spread_kernel(in_ref, out_ref):
    total = jnp.sum(in_ref[...], axis=0)
    for d in range(16):
        out_ref[d] = total


def finish_kernel(gram_ref, img_ref, out_ref, factor_ref, inv_ref):
    total = jnp.sum(gram_ref[...], axis=0) * (1.0 / CELLS)
    lane = lax.broadcasted_iota(jnp.int32, (16, 128), 1)
    row = lax.broadcasted_iota(jnp.int32, (16, 128), 0)
    g = jnp.concatenate(
        [jnp.broadcast_to(total[0:1], (8, 128)), jnp.broadcast_to(total[1:2], (8, 128))], axis=0
    )
    g = jnp.where((lane >> 4) == (row & 7), g, 0.0)
    for step in (16, 32, 64):
        g = g + pltpu.roll(g, step, 1)
    g = jnp.where(lane < 16, g, jnp.where(lane == row + 16, 1.0, 0.0))
    for k in range(PROBES - 1):
        pivot_row = jnp.broadcast_to(g[k : k + 1], (16, 128))
        column = jnp.broadcast_to(g[:, k : k + 1], (16, 128))
        pivot = jnp.broadcast_to(pivot_row[:, k : k + 1], (16, 128))
        g = g - jnp.where(row > k, column / pivot, 0.0) * pivot_row
    diagonal = jnp.sum(jnp.where(lane == row, g, 0.0), axis=1, keepdims=True)
    g = g / jnp.sqrt(diagonal)
    factor_ref[...] = jnp.where(lane >= row, g, 0.0)[:, :16]
    for j in range(PROBES):
        inv_ref[j] = jnp.broadcast_to(g[:, 16 + j : 17 + j], (16, 128))
    for i in range(PROBES):
        value = jnp.broadcast_to(inv_ref[0, i : i + 1], (64, 128)) * img_ref[0]
        for j in range(1, i + 1):
            value = value + jnp.broadcast_to(inv_ref[j, i : i + 1], (64, 128)) * img_ref[j]
        out_ref[i] = value


def call(kernel, out_shapes, scratch=(), smem=0, inputs=1, copies=0):
    out_shape = [jax.ShapeDtypeStruct(s, F32) for s in out_shapes]
    vmem = pl.BlockSpec(memory_space=pltpu.VMEM)
    given = pl.BlockSpec(memory_space=pltpu.HBM) if copies else vmem
    specs = [pl.BlockSpec(memory_space=pltpu.SMEM)] * smem + [given] * inputs
    sems = [pltpu.SemaphoreType.DMA((copies,))] if copies else []
    return pl.pallas_call(
        kernel,
        out_shape=out_shape,
        in_specs=specs,
        out_specs=[vmem] * len(out_shape),
        scratch_shapes=[pltpu.VMEM(s, F32) for s in scratch] + sems,
        compiler_params=pltpu.CompilerParams(vmem_limit_bytes=40 * 1024 * 1024),
    )


def on_device(log_perm, pressure, data_weight, probes):
    planes = [a.reshape(64, 128) for a in (log_perm, pressure, data_weight)]
    block = (64, 128)
    scratch = [block, block, block, (16, 64, 128), block, (128, 128)]
    (sent,) = call(pack_kernel, [(32, 56, 128)], scratch, inputs=4, copies=4)(
        *planes, probes.reshape(16, 64, 128)
    )
    got = lax.all_to_all(sent, ("gx", "gy"), 0, 0)
    plane, msg = (8, WIN, 8, 128), (MSG, 8, 128)
    own_s, own_c, own_w, low, high = call(
        arrange_kernel, [plane, plane, (4, WIN, 8, 128), msg, msg]
    )(got.reshape(32 * 56, 128))

    blocks = lax.axis_size("gz")
    up = []
    for q in range(4):
        route = []
        for n in range(8 * blocks):
            gx, gy = place(n // 8, n % 8, q)
            route.append((gx * 4 + gy) * blocks + n // 8)
        up += [(route[n], route[n + 1]) for n in range(len(route) - 1)]
    down = [(j, i) for i, j in up]
    from_below = lax.ppermute(high, ("gx", "gy", "gz"), up)
    from_above = lax.ppermute(low, ("gx", "gy", "gz"), down)
    block = lax.axis_index("gz")
    at_end = (lax.axis_index("gx") % 2 == 0) & (lax.axis_index("gy") == 0)
    edge = jnp.stack([at_end & (block == 0), at_end & (block == blocks - 1)]).astype(jnp.int32)
    field = (8, ROWS, 8, 128)
    far = (6, ROWS, 8, 128)
    scratch = ([field] * 3 + [far, field]) * 2
    scratch += [field] * 2 + [(8, WIN + 2 * INNER, 8, 128)] + [field] * 5
    (images,) = call(core_kernel, [(1024, 128)], scratch, smem=1, inputs=5)(
        edge, from_below, own_s, own_c, own_w, from_above
    )
    back = lax.all_to_all(images.reshape(32, 32, 128), ("gx", "gy"), 0, 0)
    image_rows, gram = call(
        gram_kernel, [(16, 64, 128), (32, 2, 128)], [(2048, 128), (2, 128, 128)]
    )(back)
    gram = lax.all_to_all(gram, ("gx", "gy"), 0, 0)
    (gram,) = call(spread_kernel, [(16, 2, 128)])(gram)
    gram = lax.all_to_all(gram, "gz", 0, 0)
    basis, factor = call(
        finish_kernel, [(16, 64, 128), (16, 16)], [(16, 16, 128)], inputs=2
    )(gram, image_rows)
    return (basis.reshape(probes.shape), factor)


def solution(mesh):
    in_specs = (
        P("gx", "gy", "gz"),
        P("gx", "gy", "gz"),
        P("gx", "gy", "gz"),
        P(None, "gx", "gy", "gz"),
    )
    out_specs = (P(None, "gx", "gy", "gz"), P())
    return jax.shard_map(
        on_device, mesh=mesh, in_specs=in_specs, out_specs=out_specs, check_vma=False
    )
```

```python
import jax
import jax.numpy as jnp
from jax import lax
from jax.experimental import pallas as pl
from jax.experimental.pallas import tpu as pltpu
from jax.sharding import PartitionSpec as P

DEG = 4
SHIFT = 0.5
LOWER = 0.5
UPPER = 33.5
MID = (UPPER + LOWER) / 2.0
HALF = (UPPER - LOWER) / 2.0
RATIO = MID / HALF

PROBES = 16
CELLS = 32 * 64 * 2048
WIN = 16
HALO = 2 * DEG + 2
INNER = DEG + 1
ROWS = WIN + 2 * HALO
UNROLL = 16
BLOCK = 7
MSG = 12 * HALO + 4 * INNER
F32 = jnp.float32

PATHS = (
    ((0, 0), (0, 1), (1, 1), (1, 2), (0, 2), (0, 3), (1, 3), (1, 0)),
    ((1, 0), (1, 1), (2, 1), (2, 2), (1, 2), (1, 3), (2, 3), (2, 0)),
)


def place(block, w, q):
    core, layer = block % 2, block // 2
    gx = (PATHS[core][w][0] + 2 * (q + layer)) % 8
    return gx, PATHS[core][w][1]


def placer():
    block = lax.axis_index("gz")
    core, layer = block % 2, block // 2

    def number(w, q):
        (x0, y0), (x1, y1) = PATHS[0][w], PATHS[1][w]
        gx = (x0 + core * (x1 - x0) + 2 * (q + layer)) % 8
        return gx * 4 + y0 + core * (y1 - y0)

    return number


def lane_sub():
    lane = lax.broadcasted_iota(jnp.int32, (8, 128), 1)
    return lane, lax.broadcasted_iota(jnp.int32, (8, 128), 0)


def swap_groups(v):
    last = v[0].ndim - 1
    lane = lax.broadcasted_iota(jnp.int32, v[0].shape, last)
    high, low = (lane & 64) == 0, (lane & 32) == 0
    u = [None] * 4
    for a in range(2):
        moved = pltpu.roll(jnp.where(high, v[a + 2], v[a]), 64, last)
        u[a] = jnp.where(high, v[a], moved)
        u[a + 2] = jnp.where(high, moved, v[a + 2])
    out = [None] * 4
    for a in (0, 2):
        out[a] = jnp.where(low, u[a], pltpu.roll(u[a + 1], 32, last))
        out[a + 1] = jnp.where(low, pltpu.roll(u[a], 96, last), u[a + 1])
    return out


def pack_kernel(
    lp_hbm, pr_hbm, dw_hbm, v_hbm, out_hbm,
    lp_ref, pr_ref, dw_ref, v_ref, perm_ref, mix_ref, out_ref, in_sems, out_sems,
):
    pairs = [(lp_hbm, lp_ref), (pr_hbm, pr_ref), (dw_hbm, dw_ref)]
    pairs += [(v_hbm.at[pl.ds(4 * q, 4)], v_ref.at[pl.ds(4 * q, 4)]) for q in range(4)]
    copies = [pltpu.make_async_copy(a, b, in_sems.at[i]) for i, (a, b) in enumerate(pairs)]
    for copy in copies:
        copy.start()
    first = (lane_sub()[0] & 2) == 0
    number = placer()
    dest = [[number(w, q) for q in range(4)] for w in range(8)]

    def mixed(parts, at):
        for slot in range(4):
            mix_ref[at, pl.ds(slot, 32, stride=4), :] = parts[slot]
        return mix_ref[at].T

    def half(ref, yl):
        return ref[pl.ds(yl, 32, stride=2), :]

    def paired(tile, w):
        return jnp.where(first, tile[16 * w : 16 * w + 8], tile[16 * w + 8 : 16 * w + 16])

    for copy in copies[:3]:
        copy.wait()
    perm_ref[...] = jnp.exp(lp_ref[...])
    perm = [half(perm_ref, yl) for yl in range(2)]
    tiles = [mixed([perm[yl], half(pr_ref, yl)] * 2, yl) for yl in range(2)]
    tiles.append(mixed([half(dw_ref, 0), half(dw_ref, 1)] * 2, 2))
    for w in range(8):
        for i in range(3):
            packed = paired(tiles[i], w)
            for q in range(4):
                out_ref[dest[w][q], 32 + 8 * i : 40 + 8 * i] = packed
    sends = []
    for q in range(4):
        copies[3 + q].wait()
        for yl in range(2):
            fields = [
                perm[yl] * v_ref[4 * q + p, pl.ds(yl, 32, stride=2), :] for p in range(4)
            ]
            tile = mixed(fields, 3 + yl)
            for w in range(8):
                out_ref[dest[w][q], 16 * yl : 16 * yl + 16] = tile[16 * w : 16 * w + 16]
        for w in range(8):
            at = dest[w][q]
            sends.append(
                pltpu.make_async_copy(out_ref.at[at], out_hbm.at[at], out_sems.at[8 * q + w])
            )
            sends[-1].start()
    for send in sends:
        send.wait()


def widen(v, first):
    last = v.ndim - 1
    return jnp.where(first, v, pltpu.roll(v, 2, last)), jnp.where(first, pltpu.roll(v, 126, last), v)


def split(v, even):
    last = v.ndim - 1
    return jnp.where(even, v, pltpu.roll(v, 1, last)), jnp.where(even, pltpu.roll(v, 127, last), v)


def arrange_kernel(in_ref, s_ref, c_ref, w_ref, low_ref, high_ref):
    first = (lane_sub()[0] & 2) == 0

    def fetch(begin, count):
        got = [
            jnp.stack([in_ref[pl.ds(56 * g + begin + k, 8, stride=224), :] for k in range(count)])
            for g in range(4)
        ]
        return swap_groups(got)

    lift, pairs = WIN - HALO, HALO // 2
    for yl in range(2):
        for begin in range(0, WIN, 8):
            for x, v in enumerate(fetch(16 * yl + begin, 8)):
                n = 4 * yl + x
                s_ref[n, begin : begin + 8] = v
                for k in range(8):
                    z = begin + k
                    if z < HALO:
                        low_ref[HALO * n + z] = v[k]
                    if z >= lift:
                        high_ref[HALO * n + z - lift] = v[k]
        for x, v in enumerate(fetch(32 + 8 * yl, 8)):
            n = 4 * yl + x
            below, above = widen(v, first)
            c_ref[n, 0:8] = below
            c_ref[n, 8:16] = above
            c = [below[z] if z < 8 else above[z - 8] for z in range(WIN)]
            for k in range(pairs):
                at = 8 * HALO + pairs * n + k
                low_ref[at] = jnp.where(first, c[k], c[k + pairs])
                high_ref[at] = jnp.where(first, c[lift + k], c[lift + k + pairs])
    for x, v in enumerate(fetch(48, 8)):
        below, above = widen(v, first)
        w_ref[x, 0:8] = below
        w_ref[x, 8:16] = above
        at = 12 * HALO + INNER * x
        low_ref[at : at + INNER] = below[:INNER]
        high_ref[at : at + INNER] = above[8 - INNER :]


def core_kernel(
    edge_ref, lo_ref, s_own_ref, c_own_ref, w_own_ref, hi_ref, out_ref,
    kx_ref, ky_ref, kz_ref, kd_ref, diag_ref, dx_ref, dy_ref, dz_ref, dd_ref, pd_ref,
    perm_ref, press_ref, wt_ref, s_ref, *e_refs,
):
    image_ref = e_refs[1]
    lane, sub = lane_sub()
    first, even = (lane & 2) == 0, (lane & 1) == 0
    at_first, at_last = edge_ref[0].astype(F32), edge_ref[1].astype(F32)

    for n in range(8):
        s_ref[n, HALO : HALO + WIN] = s_own_ref[n]
        perm, press = split(c_own_ref[n], even)
        perm_ref[n, HALO : HALO + WIN] = perm
        press_ref[n, HALO : HALO + WIN] = press
    for x in range(4):
        low, high = split(w_own_ref[x], even)
        wt_ref[x, INNER : INNER + WIN] = low
        wt_ref[4 + x, INNER : INNER + WIN] = high
    pairs = HALO // 2
    for src_ref, base, inner in ((lo_ref, 0, 0), (hi_ref, HALO + WIN, INNER + WIN)):
        for n in range(8):
            begin = HALO * n
            s_ref[n, base : base + HALO] = src_ref[begin : begin + HALO]
            begin = 8 * HALO + pairs * n
            for part, c in enumerate(widen(src_ref[begin : begin + pairs], first)):
                at = base + pairs * part
                perm, press = split(c, even)
                perm_ref[n, at : at + pairs] = perm
                press_ref[n, at : at + pairs] = press
        for x in range(4):
            begin = 12 * HALO + INNER * x
            low, high = split(src_ref[begin : begin + INNER], even)
            wt_ref[x, inner : inner + INNER] = low
            wt_ref[4 + x, inner : inner + INNER] = high

    def mark(n):
        none = jnp.zeros((8, 128), F32)
        return (
            jnp.where(sub == 0, 0.5, 0.0) if n % 4 == 0 else none,
            jnp.where(sub == 7, 0.5, 0.0) if n % 4 == 3 else none,
            jnp.where(lane < 4, 0.5, 0.0) if n < 4 else none,
            jnp.where(lane >= 124, 0.5, 0.0) if n >= 4 else none,
        )

    ends = [mark(n) for n in range(8)]

    def far(v):
        return (
            [pltpu.roll(v[n], 7, 1) for n in (0, 4)]
            + [pltpu.roll(v[n], 1, 1) for n in (3, 7)]
            + [pltpu.roll(v[n], 124, 2) for n in range(4)]
            + [pltpu.roll(v[n + 4], 4, 2) for n in range(4)]
        )

    def coefficients(step, carry):
        here, above = pl.ds(BLOCK * step, BLOCK), pl.ds(BLOCK * step + 1, BLOCK)
        perm = [perm_ref[n, here] for n in range(8)]
        press = [press_ref[n, here] for n in range(8)]
        perm_far, press_far = far(perm), far(press)
        outs = []
        for n in range(8):
            x_begin, x_end, y_begin, y_end = ends[n]
            outside = (x_begin + x_end) + (y_begin + y_end)
            half_x, half_y = 0.5 - x_end, 0.5 - y_end
            near = (n + 1, None) if n % 4 < 3 else (None, n // 4)
            for field, field_far, out_ref, sign in (
                (perm, perm_far, kx_ref, 1.0),
                (press, press_far, dx_ref, -1.0),
            ):
                up = field_far[near[1]] if near[0] is None else field[near[0]]
                outs.append((out_ref, n, half_x * (field[n] + sign * up)))
            for field, field_far, out_ref, sign in (
                (perm, perm_far, ky_ref, 1.0),
                (press, press_far, dy_ref, -1.0),
            ):
                up = field[n + 4] if n < 4 else field_far[n]
                outs.append((out_ref, n, half_y * (field[n] + sign * up)))
            outs.append((kz_ref, n, 0.5 * (perm[n] + perm_ref[n, above])))
            outs.append((dz_ref, n, 0.5 * (press[n] - press_ref[n, above])))
            outs.append((diag_ref, n, SHIFT + outside * perm[n]))
            outs.append((pd_ref, n, outside * press[n]))
        for i, n in enumerate((0, 4, 0, 1, 2, 3)):
            half = 0.5 - ends[n][0 if i < 2 else 2]
            at = 2 + i if i < 2 else 6 + i
            outs.append((kd_ref, i, half * (perm[n] + perm_far[at])))
            outs.append((dd_ref, i, half * (press_far[at] - press[n])))
        for ref, n, value in outs:
            ref[n, here] = value
        return carry

    lax.fori_loop(0, (ROWS - 1) // BLOCK, coefficients, 0)
    for row, inside, end in ((HALO - 1, HALO, at_first), (HALO + WIN - 1, HALO + WIN - 1, at_last)):
        for n in range(8):
            kz_ref[n, row] = kz_ref[n, row] * (1.0 - end)
            dz_ref[n, row] = dz_ref[n, row] * (1.0 - end)
            diag_ref[n, inside] = diag_ref[n, inside] + (0.5 * end) * perm_ref[n, inside]
            pd_ref[n, inside] = pd_ref[n, inside] + (0.5 * end) * press_ref[n, inside]

    def sweep(field_ref, begin, end, face_refs, centre_ref, join, sign, inputs, finish):
        fx_ref, fy_ref, fz_ref, fd_ref = face_refs

        def part(up, down):
            return up - down if sign < 0 else up + down

        def rows(row, count):
            here, below = pl.ds(row, count), pl.ds(row - 1, count + 1)
            now = [field_ref[n, here] for n in range(8)]
            around = far(now)
            flow_x, back_x, flow_y, back_y = ([None] * 8 for _ in range(4))
            for n in range(8):
                up = now[n + 1] if n % 4 < 3 else around[n // 4]
                flow_x[n] = join(now[n], up) * fx_ref[n, here]
                up = now[n + 4] if n < 4 else around[n]
                flow_y[n] = join(now[n], up) * fy_ref[n, here]
            for n in range(8):
                if n % 4:
                    back_x[n] = flow_x[n - 1]
                else:
                    back_x[n] = join(around[2 + n // 4], now[n]) * fd_ref[n // 4, here]
                if n >= 4:
                    back_y[n] = flow_y[n - 4]
                else:
                    back_y[n] = join(around[8 + n], now[n]) * fd_ref[2 + n, here]
            results = []
            for n in range(8):
                flow_z = join(field_ref[n, below], field_ref[n, pl.ds(row, count + 1)])
                flow_z = flow_z * fz_ref[n, below]
                total = centre_ref[n, here] * now[n] + part(flow_x[n], back_x[n])
                total = total + (part(flow_y[n], back_y[n]) + part(flow_z[1:], flow_z[:-1]))
                extra = [ref[n, here] for ref in inputs]
                results.append((n, finish(row, count, n, now[n], total, *extra)))
            for n, outs in results:
                for ref, value in outs:
                    ref[n, here] = value

        steps, rest = divmod(end - begin, UNROLL)

        def body(i, carry):
            rows(begin + UNROLL * i, UNROLL)
            return carry

        lax.fori_loop(0, steps, body, 0)
        if rest:
            rows(end - rest, rest)

    def add(a, b):
        return a + b

    def minus(a, b):
        return a - b

    def solve(lowest, finish_last):
        keep_now, take_now, weight_now = 0.0, 1.0 / MID, 1.0 / RATIO
        for repeat in range(DEG):
            weight_next = 1.0 / (2.0 * RATIO - weight_now)
            keep, take = weight_next * weight_now, 2.0 * weight_next / HALF
            grow, drop = keep + take / take_now, take * keep_now / take_now
            keep_now, take_now, weight_now = keep, take, weight_next
            last = repeat == DEG - 1

            def finish(row, count, n, v, total, *old, grow=grow, drop=drop, take=take, i=repeat):
                direction = grow * v - take * total
                if i:
                    direction = direction - drop * old[0]
                if i < DEG - 1:
                    return [(e_refs[i + 1], direction)]
                iterate = direction + v
                for e in old:
                    iterate = iterate + e
                return finish_last(row, count, n, iterate)

            old = e_refs[repeat - 1 :: -1] if last else e_refs[repeat - 1 : repeat]
            begin = lowest + 1 + repeat
            faces = (kx_ref, ky_ref, kz_ref, kd_ref)
            sweep(
                e_refs[repeat], begin, ROWS - begin, faces, diag_ref, minus, -1,
                old if repeat else (), finish,
            )

    faces = (dx_ref, dy_ref, dz_ref, dd_ref)

    def start(row, count, n, v, total):
        return [(e_refs[0], total * (1.0 / MID))]

    sweep(s_ref, 1, ROWS - 1, faces, pd_ref, add, -1, (), start)
    skip = HALO - INNER

    def second(row, count, n, value):
        return [(e_refs[0], value * (wt_ref[n, pl.ds(row - skip, count)] * (1.0 / MID)))]

    solve(1, second)
    solve(skip, lambda row, count, n, value: [(s_ref, value)])

    def image(row, count, n, v, total):
        return [(image_ref, perm_ref[n, pl.ds(row, count)] * total)]

    sweep(s_ref, HALO, HALO + WIN, faces, pd_ref, minus, 1, (), image)

    for yl in range(2):
        for begin in range(0, WIN, 8):
            at = slice(HALO + begin, HALO + begin + 8)
            v = swap_groups([image_ref[4 * yl + x, at] for x in range(4)])
            for g in range(4):
                for k in range(8):
                    to = g * 2 * WIN + yl * WIN + begin + k
                    out_ref[pl.ds(to, 8, stride=8 * WIN), :] = v[g][k]


def gram_kernel(in_ref, img_ref, gram_ref, acc_ref, mix_ref):
    number = placer()
    for q in range(4):
        source = [number(w, q) for w in range(8)]
        for yl in range(2):
            rows = [in_ref[source[w], 16 * yl : 16 * yl + 16] for w in range(8)]
            mix_ref[yl] = jnp.concatenate(rows, axis=0).T
            for p in range(4):
                img_ref[4 * q + p, pl.ds(yl, 32, stride=2), :] = mix_ref[
                    yl, pl.ds(p, 32, stride=4), :
                ]
    for i in range(PROBES):
        a = [img_ref[i, 8 * k : 8 * k + 8] for k in range(8)]
        for j in range(i + 1):
            parts = [a[k] * img_ref[j, 8 * k : 8 * k + 8] for k in range(8)]
            while len(parts) > 1:
                parts = [parts[k] + parts[k + 1] for k in range(0, len(parts), 2)]
            begin = (16 * i + j) * 8
            acc_ref[begin : begin + 8] = parts[0]
            begin = (16 * j + i) * 8
            acc_ref[begin : begin + 8] = parts[0]
    sums = []
    for c in range(32):
        parts = [acc_ref[pl.ds(64 * c + s, 8, stride=8), :] for s in range(8)]
        while len(parts) > 1:
            parts = [parts[k] + parts[k + 1] for k in range(0, len(parts), 2)]
        sums.append(parts[0])
    total = lax.dot_general(
        jnp.ones((8, 128), F32),
        jnp.concatenate(sums, axis=0),
        (((1,), (1,)), ((), ())),
        precision=lax.Precision.HIGHEST,
        preferred_element_type=F32,
    )
    _, sub = lane_sub()
    tile = jnp.where(sub == 0, total[:, :128], total[:, 128:])
    for d in range(32):
        gram_ref[d] = tile[0:2]


def spread_kernel(in_ref, out_ref):
    total = jnp.sum(in_ref[...], axis=0)
    for d in range(16):
        out_ref[d] = total


def finish_kernel(gram_ref, img_ref, out_hbm, factor_ref, inv_ref, out_ref, sems):
    total = jnp.sum(gram_ref[...], axis=0) * (1.0 / CELLS)
    lane = lax.broadcasted_iota(jnp.int32, (16, 128), 1)
    row = lax.broadcasted_iota(jnp.int32, (16, 128), 0)
    g = jnp.concatenate(
        [jnp.broadcast_to(total[0:1], (8, 128)), jnp.broadcast_to(total[1:2], (8, 128))], axis=0
    )
    g = jnp.where((lane >> 4) == (row & 7), g, 0.0)
    for step in (16, 32, 64):
        g = g + pltpu.roll(g, step, 1)
    column = [jnp.broadcast_to(g[:, j : j + 1], (16, 128)) for j in range(PROBES)]
    inverse = [jnp.where(row == j, 1.0, 0.0) for j in range(PROBES)]
    pivots = jnp.ones((16, 128), F32)
    for k in range(PROBES):
        pivot = jnp.broadcast_to(column[k][k : k + 1], (16, 128))
        pivots = jnp.where(row == k, pivot, pivots)
        ratio = jnp.where(row > k, column[k] / pivot, 0.0)
        for j in range(k + 1, PROBES):
            column[j] = column[j] - ratio * jnp.broadcast_to(column[j][k : k + 1], (16, 128))
        for j in range(k + 1):
            inverse[j] = inverse[j] - ratio * jnp.broadcast_to(inverse[j][k : k + 1], (16, 128))
    scale = 1.0 / jnp.sqrt(pivots)
    factor = jnp.zeros((16, 128), F32)
    for j in range(PROBES):
        factor = jnp.where((lane == j) & (row <= j), column[j] * scale, factor)
        inv_ref[j] = inverse[j] * scale
    factor_ref[...] = factor[:, :16]
    for i in range(PROBES):
        value = jnp.broadcast_to(inv_ref[0, i : i + 1], (64, 128)) * img_ref[0]
        for j in range(1, i + 1):
            value = value + jnp.broadcast_to(inv_ref[j, i : i + 1], (64, 128)) * img_ref[j]
        out_ref[i] = value
        pltpu.make_async_copy(out_ref.at[i], out_hbm.at[i], sems.at[i]).start()
    for i in range(PROBES):
        pltpu.make_async_copy(out_ref.at[i], out_hbm.at[i], sems.at[i]).wait()


def call(kernel, out_shapes, scratch=(), smem=0, inputs=1, copies=(), limit=40):
    out_shape = [jax.ShapeDtypeStruct(s, F32) for s in out_shapes]
    vmem = pl.BlockSpec(memory_space=pltpu.VMEM)
    hbm = pl.BlockSpec(memory_space=pl.ANY)
    specs = [pl.BlockSpec(memory_space=pltpu.SMEM)] * smem
    specs += [hbm if len(copies) == 2 else vmem] * inputs
    return pl.pallas_call(
        kernel,
        out_shape=out_shape,
        in_specs=specs,
        out_specs=[hbm if copies else vmem] + [vmem] * (len(out_shape) - 1),
        scratch_shapes=[pltpu.VMEM(s, F32) for s in scratch]
        + [pltpu.SemaphoreType.DMA((n,)) for n in copies],
        compiler_params=pltpu.CompilerParams(vmem_limit_bytes=limit * 1024 * 1024),
    )


def on_device(log_perm, pressure, data_weight, probes):
    planes = [a.reshape(64, 128) for a in (log_perm, pressure, data_weight)]
    block = (64, 128)
    scratch = [block, block, block, (16, 64, 128), block, (5, 128, 128), (32, 56, 128)]
    (sent,) = call(pack_kernel, [(32, 56, 128)], scratch, inputs=4, copies=(7, 32), limit=60)(
        *planes, probes.reshape(16, 64, 128)
    )
    got = lax.all_to_all(sent, ("gx", "gy"), 0, 0)
    plane, msg = (8, WIN, 8, 128), (MSG, 8, 128)
    own_s, own_c, own_w, low, high = call(
        arrange_kernel, [plane, plane, (4, WIN, 8, 128), msg, msg]
    )(got.reshape(32 * 56, 128))

    blocks = lax.axis_size("gz")
    up = []
    for q in range(4):
        route = []
        for n in range(8 * blocks):
            gx, gy = place(n // 8, n % 8, q)
            route.append((gx * 4 + gy) * blocks + n // 8)
        up += [(route[n], route[n + 1]) for n in range(len(route) - 1)]
    down = [(j, i) for i, j in up]
    from_below = lax.ppermute(high, ("gx", "gy", "gz"), up)
    from_above = lax.ppermute(low, ("gx", "gy", "gz"), down)
    block = lax.axis_index("gz")
    at_end = (lax.axis_index("gx") % 2 == 0) & (lax.axis_index("gy") == 0)
    edge = jnp.stack([at_end & (block == 0), at_end & (block == blocks - 1)]).astype(jnp.int32)
    field = (8, ROWS, 8, 128)
    far = (6, ROWS, 8, 128)
    scratch = ([field] * 3 + [far, field]) * 2
    scratch += [field] * 2 + [(8, WIN + 2 * INNER, 8, 128)] + [field] * 5
    (images,) = call(core_kernel, [(1024, 128)], scratch, smem=1, inputs=5)(
        edge, from_below, own_s, own_c, own_w, from_above
    )
    back = lax.all_to_all(images.reshape(32, 32, 128), ("gx", "gy"), 0, 0)
    image_rows, gram = call(
        gram_kernel, [(16, 64, 128), (32, 2, 128)], [(2048, 128), (2, 128, 128)]
    )(back)
    gram = lax.all_to_all(gram, ("gx", "gy"), 0, 0)
    (gram,) = call(spread_kernel, [(16, 2, 128)])(gram)
    gram = lax.all_to_all(gram, "gz", 0, 0)
    basis, factor = call(
        finish_kernel,
        [(16, 64, 128), (16, 16)],
        [(16, 16, 128), (16, 64, 128)],
        inputs=2,
        copies=(16,),
    )(gram, image_rows)
    return (basis.reshape(probes.shape), factor)


def solution(mesh):
    in_specs = (
        P("gx", "gy", "gz"),
        P("gx", "gy", "gz"),
        P("gx", "gy", "gz"),
        P(None, "gx", "gy", "gz"),
    )
    out_specs = (P(None, "gx", "gy", "gz"), P())
    return jax.shard_map(
        on_device, mesh=mesh, in_specs=in_specs, out_specs=out_specs, check_vma=False
    )
```

```python
import jax
import jax.numpy as jnp
from jax import lax
from jax.experimental import pallas as pl
from jax.experimental.pallas import tpu as pltpu
from jax.sharding import PartitionSpec as P

DEG = 4
SHIFT = 0.5
LOWER = 0.5
UPPER = 33.5
MID = (UPPER + LOWER) / 2.0
HALF = (UPPER - LOWER) / 2.0
RATIO = MID / HALF

PROBES = 16
CELLS = 32 * 64 * 2048
WIN = 16
HALO = 2 * DEG + 2
INNER = DEG + 1
ROWS = WIN + 2 * HALO
UNROLL = 16
BLOCK = 7
MSG = 12 * HALO + 4 * INNER
F32 = jnp.float32

PATHS = (
    ((0, 0), (0, 1), (1, 1), (1, 2), (0, 2), (0, 3), (1, 3), (1, 0)),
    ((1, 0), (1, 1), (2, 1), (2, 2), (1, 2), (1, 3), (2, 3), (2, 0)),
)


def place(block, w, q):
    core, layer = block % 2, block // 2
    gx = (PATHS[core][w][0] + 2 * (q + layer)) % 8
    return gx, PATHS[core][w][1]


def placer():
    block = lax.axis_index("gz")
    core, layer = block % 2, block // 2

    def number(w, q):
        (x0, y0), (x1, y1) = PATHS[0][w], PATHS[1][w]
        gx = (x0 + core * (x1 - x0) + 2 * (q + layer)) % 8
        return gx * 4 + y0 + core * (y1 - y0)

    return number


def lane_sub():
    lane = lax.broadcasted_iota(jnp.int32, (8, 128), 1)
    return lane, lax.broadcasted_iota(jnp.int32, (8, 128), 0)


def swap_groups(v):
    last = v[0].ndim - 1
    lane = lax.broadcasted_iota(jnp.int32, v[0].shape, last)
    high, low = (lane & 64) == 0, (lane & 32) == 0
    u = [None] * 4
    for a in range(2):
        moved = pltpu.roll(jnp.where(high, v[a + 2], v[a]), 64, last)
        u[a] = jnp.where(high, v[a], moved)
        u[a + 2] = jnp.where(high, moved, v[a + 2])
    out = [None] * 4
    for a in (0, 2):
        out[a] = jnp.where(low, u[a], pltpu.roll(u[a + 1], 32, last))
        out[a + 1] = jnp.where(low, pltpu.roll(u[a], 96, last), u[a + 1])
    return out


def pack_kernel(
    lp_hbm, pr_hbm, dw_hbm, v_hbm, out_ref,
    lp_ref, pr_ref, dw_ref, v_ref, perm_ref, mix_ref, in_sems,
):
    pairs = [(lp_hbm, lp_ref), (pr_hbm, pr_ref), (dw_hbm, dw_ref)]
    pairs += [(v_hbm.at[pl.ds(4 * q, 4)], v_ref.at[pl.ds(4 * q, 4)]) for q in range(4)]
    copies = [pltpu.make_async_copy(a, b, in_sems.at[i]) for i, (a, b) in enumerate(pairs)]
    for copy in copies:
        copy.start()
    first = (lane_sub()[0] & 2) == 0
    number = placer()
    dest = [[number(w, q) for q in range(4)] for w in range(8)]

    def mixed(parts, at):
        for slot in range(4):
            mix_ref[at, pl.ds(slot, 32, stride=4), :] = parts[slot]
        return mix_ref[at].T

    def half(ref, yl):
        return ref[pl.ds(yl, 32, stride=2), :]

    def paired(tile, w):
        return jnp.where(first, tile[16 * w : 16 * w + 8], tile[16 * w + 8 : 16 * w + 16])

    for copy in copies[:3]:
        copy.wait()
    perm_ref[...] = jnp.exp(lp_ref[...])
    perm = [half(perm_ref, yl) for yl in range(2)]
    tiles = [mixed([perm[yl], half(pr_ref, yl)] * 2, yl) for yl in range(2)]
    tiles.append(mixed([half(dw_ref, 0), half(dw_ref, 1)] * 2, 2))
    for w in range(8):
        for i in range(3):
            packed = paired(tiles[i], w)
            for q in range(4):
                out_ref[dest[w][q], 32 + 8 * i : 40 + 8 * i] = packed
    for q in range(4):
        copies[3 + q].wait()
        for yl in range(2):
            fields = [
                perm[yl] * v_ref[4 * q + p, pl.ds(yl, 32, stride=2), :] for p in range(4)
            ]
            tile = mixed(fields, 3 + yl)
            for w in range(8):
                out_ref[dest[w][q], 16 * yl : 16 * yl + 16] = tile[16 * w : 16 * w + 16]


def widen(v, first):
    last = v.ndim - 1
    return jnp.where(first, v, pltpu.roll(v, 2, last)), jnp.where(first, pltpu.roll(v, 126, last), v)


def split(v, even):
    last = v.ndim - 1
    return jnp.where(even, v, pltpu.roll(v, 1, last)), jnp.where(even, pltpu.roll(v, 127, last), v)


def arrange_kernel(in_ref, s_ref, c_ref, w_ref, low_ref, high_ref):
    first = (lane_sub()[0] & 2) == 0

    def fetch(begin, count):
        got = [
            jnp.stack([in_ref[pl.ds(56 * g + begin + k, 8, stride=224), :] for k in range(count)])
            for g in range(4)
        ]
        return swap_groups(got)

    lift, pairs = WIN - HALO, HALO // 2
    for yl in range(2):
        for begin in range(0, WIN, 8):
            for x, v in enumerate(fetch(16 * yl + begin, 8)):
                n = 4 * yl + x
                s_ref[n, begin : begin + 8] = v
                for k in range(8):
                    z = begin + k
                    if z < HALO:
                        low_ref[HALO * n + z] = v[k]
                    if z >= lift:
                        high_ref[HALO * n + z - lift] = v[k]
        for x, v in enumerate(fetch(32 + 8 * yl, 8)):
            n = 4 * yl + x
            below, above = widen(v, first)
            c_ref[n, 0:8] = below
            c_ref[n, 8:16] = above
            c = [below[z] if z < 8 else above[z - 8] for z in range(WIN)]
            for k in range(pairs):
                at = 8 * HALO + pairs * n + k
                low_ref[at] = jnp.where(first, c[k], c[k + pairs])
                high_ref[at] = jnp.where(first, c[lift + k], c[lift + k + pairs])
    for x, v in enumerate(fetch(48, 8)):
        below, above = widen(v, first)
        w_ref[x, 0:8] = below
        w_ref[x, 8:16] = above
        at = 12 * HALO + INNER * x
        low_ref[at : at + INNER] = below[:INNER]
        high_ref[at : at + INNER] = above[8 - INNER :]


def core_kernel(
    edge_ref, lo_ref, s_own_ref, c_own_ref, w_own_ref, hi_ref, out_ref,
    kx_ref, ky_ref, kz_ref, kd_ref, diag_ref, dx_ref, dy_ref, dz_ref, dd_ref, pd_ref,
    perm_ref, press_ref, wt_ref, s_ref, *e_refs,
):
    image_ref = e_refs[1]
    lane, sub = lane_sub()
    first, even = (lane & 2) == 0, (lane & 1) == 0
    at_first, at_last = edge_ref[0].astype(F32), edge_ref[1].astype(F32)

    for n in range(8):
        s_ref[n, HALO : HALO + WIN] = s_own_ref[n]
        perm, press = split(c_own_ref[n], even)
        perm_ref[n, HALO : HALO + WIN] = perm
        press_ref[n, HALO : HALO + WIN] = press
    for x in range(4):
        low, high = split(w_own_ref[x], even)
        wt_ref[x, INNER : INNER + WIN] = low
        wt_ref[4 + x, INNER : INNER + WIN] = high
    pairs = HALO // 2
    for src_ref, base, inner in ((lo_ref, 0, 0), (hi_ref, HALO + WIN, INNER + WIN)):
        for n in range(8):
            begin = HALO * n
            s_ref[n, base : base + HALO] = src_ref[begin : begin + HALO]
            begin = 8 * HALO + pairs * n
            for part, c in enumerate(widen(src_ref[begin : begin + pairs], first)):
                at = base + pairs * part
                perm, press = split(c, even)
                perm_ref[n, at : at + pairs] = perm
                press_ref[n, at : at + pairs] = press
        for x in range(4):
            begin = 12 * HALO + INNER * x
            low, high = split(src_ref[begin : begin + INNER], even)
            wt_ref[x, inner : inner + INNER] = low
            wt_ref[4 + x, inner : inner + INNER] = high

    def mark(n):
        none = jnp.zeros((8, 128), F32)
        return (
            jnp.where(sub == 0, 0.5, 0.0) if n % 4 == 0 else none,
            jnp.where(sub == 7, 0.5, 0.0) if n % 4 == 3 else none,
            jnp.where(lane < 4, 0.5, 0.0) if n < 4 else none,
            jnp.where(lane >= 124, 0.5, 0.0) if n >= 4 else none,
        )

    ends = [mark(n) for n in range(8)]

    def far(v):
        return (
            [pltpu.roll(v[n], 7, 1) for n in (0, 4)]
            + [pltpu.roll(v[n], 1, 1) for n in (3, 7)]
            + [pltpu.roll(v[n], 124, 2) for n in range(4)]
            + [pltpu.roll(v[n + 4], 4, 2) for n in range(4)]
        )

    def coefficients(step, carry):
        here, above = pl.ds(BLOCK * step, BLOCK), pl.ds(BLOCK * step + 1, BLOCK)
        perm = [perm_ref[n, here] for n in range(8)]
        press = [press_ref[n, here] for n in range(8)]
        perm_far, press_far = far(perm), far(press)
        outs = []
        for n in range(8):
            x_begin, x_end, y_begin, y_end = ends[n]
            outside = (x_begin + x_end) + (y_begin + y_end)
            half_x, half_y = 0.5 - x_end, 0.5 - y_end
            near = (n + 1, None) if n % 4 < 3 else (None, n // 4)
            for field, field_far, out_ref, sign in (
                (perm, perm_far, kx_ref, 1.0),
                (press, press_far, dx_ref, -1.0),
            ):
                up = field_far[near[1]] if near[0] is None else field[near[0]]
                outs.append((out_ref, n, half_x * (field[n] + sign * up)))
            for field, field_far, out_ref, sign in (
                (perm, perm_far, ky_ref, 1.0),
                (press, press_far, dy_ref, -1.0),
            ):
                up = field[n + 4] if n < 4 else field_far[n]
                outs.append((out_ref, n, half_y * (field[n] + sign * up)))
            outs.append((kz_ref, n, 0.5 * (perm[n] + perm_ref[n, above])))
            outs.append((dz_ref, n, 0.5 * (press[n] - press_ref[n, above])))
            outs.append((diag_ref, n, SHIFT + outside * perm[n]))
            outs.append((pd_ref, n, outside * press[n]))
        for i, n in enumerate((0, 4, 0, 1, 2, 3)):
            half = 0.5 - ends[n][0 if i < 2 else 2]
            at = 2 + i if i < 2 else 6 + i
            outs.append((kd_ref, i, half * (perm[n] + perm_far[at])))
            outs.append((dd_ref, i, half * (press_far[at] - press[n])))
        for ref, n, value in outs:
            ref[n, here] = value
        return carry

    lax.fori_loop(0, (ROWS - 1) // BLOCK, coefficients, 0)
    for row, inside, end in ((HALO - 1, HALO, at_first), (HALO + WIN - 1, HALO + WIN - 1, at_last)):
        for n in range(8):
            kz_ref[n, row] = kz_ref[n, row] * (1.0 - end)
            dz_ref[n, row] = dz_ref[n, row] * (1.0 - end)
            diag_ref[n, inside] = diag_ref[n, inside] + (0.5 * end) * perm_ref[n, inside]
            pd_ref[n, inside] = pd_ref[n, inside] + (0.5 * end) * press_ref[n, inside]

    def sweep(field_ref, begin, end, face_refs, centre_ref, join, sign, inputs, finish):
        fx_ref, fy_ref, fz_ref, fd_ref = face_refs

        def part(up, down):
            return up - down if sign < 0 else up + down

        def rows(row, count):
            here, below = pl.ds(row, count), pl.ds(row - 1, count + 1)
            now = [field_ref[n, here] for n in range(8)]
            around = far(now)
            flow_x, back_x, flow_y, back_y = ([None] * 8 for _ in range(4))
            for n in range(8):
                up = now[n + 1] if n % 4 < 3 else around[n // 4]
                flow_x[n] = join(now[n], up) * fx_ref[n, here]
                up = now[n + 4] if n < 4 else around[n]
                flow_y[n] = join(now[n], up) * fy_ref[n, here]
            for n in range(8):
                if n % 4:
                    back_x[n] = flow_x[n - 1]
                else:
                    back_x[n] = join(around[2 + n // 4], now[n]) * fd_ref[n // 4, here]
                if n >= 4:
                    back_y[n] = flow_y[n - 4]
                else:
                    back_y[n] = join(around[8 + n], now[n]) * fd_ref[2 + n, here]
            results = []
            for n in range(8):
                flow_z = join(field_ref[n, below], field_ref[n, pl.ds(row, count + 1)])
                flow_z = flow_z * fz_ref[n, below]
                total = centre_ref[n, here] * now[n] + part(flow_x[n], back_x[n])
                total = total + (part(flow_y[n], back_y[n]) + part(flow_z[1:], flow_z[:-1]))
                extra = [ref[n, here] for ref in inputs]
                results.append((n, finish(row, count, n, now[n], total, *extra)))
            for n, outs in results:
                for ref, value in outs:
                    ref[n, here] = value

        steps, rest = divmod(end - begin, UNROLL)

        def body(i, carry):
            rows(begin + UNROLL * i, UNROLL)
            return carry

        lax.fori_loop(0, steps, body, 0)
        if rest:
            rows(end - rest, rest)

    def add(a, b):
        return a + b

    def minus(a, b):
        return a - b

    def solve(lowest, finish_last):
        keep_now, take_now, weight_now = 0.0, 1.0 / MID, 1.0 / RATIO
        for repeat in range(DEG):
            weight_next = 1.0 / (2.0 * RATIO - weight_now)
            keep, take = weight_next * weight_now, 2.0 * weight_next / HALF
            grow, drop = keep + take / take_now, take * keep_now / take_now
            keep_now, take_now, weight_now = keep, take, weight_next
            last = repeat == DEG - 1

            def finish(row, count, n, v, total, *old, grow=grow, drop=drop, take=take, i=repeat):
                direction = grow * v - take * total
                if i:
                    direction = direction - drop * old[0]
                if i < DEG - 1:
                    return [(e_refs[i + 1], direction)]
                iterate = direction + v
                for e in old:
                    iterate = iterate + e
                return finish_last(row, count, n, iterate)

            old = e_refs[repeat - 1 :: -1] if last else e_refs[repeat - 1 : repeat]
            begin = lowest + 1 + repeat
            faces = (kx_ref, ky_ref, kz_ref, kd_ref)
            sweep(
                e_refs[repeat], begin, ROWS - begin, faces, diag_ref, minus, -1,
                old if repeat else (), finish,
            )

    faces = (dx_ref, dy_ref, dz_ref, dd_ref)

    def start(row, count, n, v, total):
        return [(e_refs[0], total * (1.0 / MID))]

    sweep(s_ref, 1, ROWS - 1, faces, pd_ref, add, -1, (), start)
    skip = HALO - INNER

    def second(row, count, n, value):
        return [(e_refs[0], value * (wt_ref[n, pl.ds(row - skip, count)] * (1.0 / MID)))]

    solve(1, second)
    solve(skip, lambda row, count, n, value: [(s_ref, value)])

    def image(row, count, n, v, total):
        return [(image_ref, perm_ref[n, pl.ds(row, count)] * total)]

    sweep(s_ref, HALO, HALO + WIN, faces, pd_ref, minus, 1, (), image)

    for yl in range(2):
        for begin in range(0, WIN, 8):
            at = slice(HALO + begin, HALO + begin + 8)
            v = swap_groups([image_ref[4 * yl + x, at] for x in range(4)])
            for g in range(4):
                for k in range(8):
                    to = g * 2 * WIN + yl * WIN + begin + k
                    out_ref[pl.ds(to, 8, stride=8 * WIN), :] = v[g][k]


def gram_kernel(in_ref, img_ref, gram_ref, acc_ref, mix_ref):
    number = placer()
    for q in range(4):
        source = [number(w, q) for w in range(8)]
        for yl in range(2):
            rows = [in_ref[source[w], 16 * yl : 16 * yl + 16] for w in range(8)]
            mix_ref[yl] = jnp.concatenate(rows, axis=0).T
            for p in range(4):
                img_ref[4 * q + p, pl.ds(yl, 32, stride=2), :] = mix_ref[
                    yl, pl.ds(p, 32, stride=4), :
                ]
    for i in range(PROBES):
        a = [img_ref[i, 8 * k : 8 * k + 8] for k in range(8)]
        for j in range(i + 1):
            parts = [a[k] * img_ref[j, 8 * k : 8 * k + 8] for k in range(8)]
            while len(parts) > 1:
                parts = [parts[k] + parts[k + 1] for k in range(0, len(parts), 2)]
            begin = (16 * i + j) * 8
            acc_ref[begin : begin + 8] = parts[0]
            begin = (16 * j + i) * 8
            acc_ref[begin : begin + 8] = parts[0]
    sums = []
    for c in range(32):
        parts = [acc_ref[pl.ds(64 * c + s, 8, stride=8), :] for s in range(8)]
        while len(parts) > 1:
            parts = [parts[k] + parts[k + 1] for k in range(0, len(parts), 2)]
        sums.append(parts[0])
    total = lax.dot_general(
        jnp.ones((8, 128), F32),
        jnp.concatenate(sums, axis=0),
        (((1,), (1,)), ((), ())),
        precision=lax.Precision.HIGHEST,
        preferred_element_type=F32,
    )
    _, sub = lane_sub()
    tile = jnp.where(sub == 0, total[:, :128], total[:, 128:])
    for d in range(32):
        gram_ref[d] = tile[0:2]


def spread_kernel(in_ref, out_ref):
    total = jnp.sum(in_ref[...], axis=0)
    for d in range(16):
        out_ref[d] = total


def finish_kernel(gram_ref, img_ref, out_hbm, factor_ref, inv_ref, out_ref, sems):
    total = jnp.sum(gram_ref[...], axis=0) * (1.0 / CELLS)
    lane = lax.broadcasted_iota(jnp.int32, (16, 128), 1)
    row = lax.broadcasted_iota(jnp.int32, (16, 128), 0)
    g = jnp.concatenate(
        [jnp.broadcast_to(total[0:1], (8, 128)), jnp.broadcast_to(total[1:2], (8, 128))], axis=0
    )
    g = jnp.where((lane >> 4) == (row & 7), g, 0.0)
    for step in (16, 32, 64):
        g = g + pltpu.roll(g, step, 1)
    column = [jnp.broadcast_to(g[:, j : j + 1], (16, 128)) for j in range(PROBES)]
    inverse = [jnp.where(row == j, 1.0, 0.0) for j in range(PROBES)]
    pivots = jnp.ones((16, 128), F32)
    for k in range(PROBES):
        pivot = jnp.broadcast_to(column[k][k : k + 1], (16, 128))
        pivots = jnp.where(row == k, pivot, pivots)
        ratio = jnp.where(row > k, column[k] / pivot, 0.0)
        for j in range(k + 1, PROBES):
            column[j] = column[j] - ratio * jnp.broadcast_to(column[j][k : k + 1], (16, 128))
        for j in range(k + 1):
            inverse[j] = inverse[j] - ratio * jnp.broadcast_to(inverse[j][k : k + 1], (16, 128))
    scale = 1.0 / jnp.sqrt(pivots)
    factor = jnp.zeros((16, 128), F32)
    for j in range(PROBES):
        factor = jnp.where((lane == j) & (row <= j), column[j] * scale, factor)
        inv_ref[j] = inverse[j] * scale
    factor_ref[...] = factor[:, :16]
    for i in range(PROBES):
        value = jnp.broadcast_to(inv_ref[0, i : i + 1], (64, 128)) * img_ref[0]
        for j in range(1, i + 1):
            value = value + jnp.broadcast_to(inv_ref[j, i : i + 1], (64, 128)) * img_ref[j]
        out_ref[i] = value
        pltpu.make_async_copy(out_ref.at[i], out_hbm.at[i], sems.at[i]).start()
    for i in range(PROBES):
        pltpu.make_async_copy(out_ref.at[i], out_hbm.at[i], sems.at[i]).wait()


def call(kernel, out_shapes, scratch=(), smem=0, inputs=1, fetch=0, send=0):
    out_shape = [jax.ShapeDtypeStruct(s, F32) for s in out_shapes]
    vmem = pl.BlockSpec(memory_space=pltpu.VMEM)
    hbm = pl.BlockSpec(memory_space=pl.ANY)
    specs = [pl.BlockSpec(memory_space=pltpu.SMEM)] * smem + [hbm if fetch else vmem] * inputs
    return pl.pallas_call(
        kernel,
        out_shape=out_shape,
        in_specs=specs,
        out_specs=[hbm if send else vmem] + [vmem] * (len(out_shape) - 1),
        scratch_shapes=[pltpu.VMEM(s, F32) for s in scratch]
        + [pltpu.SemaphoreType.DMA((n,)) for n in (fetch, send) if n],
        compiler_params=pltpu.CompilerParams(vmem_limit_bytes=40 * 1024 * 1024),
    )


def on_device(log_perm, pressure, data_weight, probes):
    planes = [a.reshape(64, 128) for a in (log_perm, pressure, data_weight)]
    block = (64, 128)
    scratch = [block, block, block, (16, 64, 128), block, (5, 128, 128)]
    fields = [*planes, probes.reshape(16, 64, 128)]
    (sent,) = call(pack_kernel, [(32, 56, 128)], scratch, inputs=4, fetch=7)(
        *[pltpu.with_memory_space_constraint(a, pltpu.HBM) for a in fields]
    )
    got = lax.all_to_all(sent, ("gx", "gy"), 0, 0)
    plane, msg = (8, WIN, 8, 128), (MSG, 8, 128)
    own_s, own_c, own_w, low, high = call(
        arrange_kernel, [plane, plane, (4, WIN, 8, 128), msg, msg]
    )(got.reshape(32 * 56, 128))

    blocks = lax.axis_size("gz")
    up = []
    for q in range(4):
        route = []
        for n in range(8 * blocks):
            gx, gy = place(n // 8, n % 8, q)
            route.append((gx * 4 + gy) * blocks + n // 8)
        up += [(route[n], route[n + 1]) for n in range(len(route) - 1)]
    down = [(j, i) for i, j in up]
    from_below = lax.ppermute(high, ("gx", "gy", "gz"), up)
    from_above = lax.ppermute(low, ("gx", "gy", "gz"), down)
    block = lax.axis_index("gz")
    at_end = (lax.axis_index("gx") % 2 == 0) & (lax.axis_index("gy") == 0)
    edge = jnp.stack([at_end & (block == 0), at_end & (block == blocks - 1)]).astype(jnp.int32)
    field = (8, ROWS, 8, 128)
    far = (6, ROWS, 8, 128)
    scratch = ([field] * 3 + [far, field]) * 2
    scratch += [field] * 2 + [(8, WIN + 2 * INNER, 8, 128)] + [field] * 5
    (images,) = call(core_kernel, [(1024, 128)], scratch, smem=1, inputs=5)(
        edge, from_below, own_s, own_c, own_w, from_above
    )
    back = lax.all_to_all(images.reshape(32, 32, 128), ("gx", "gy"), 0, 0)
    image_rows, gram = call(
        gram_kernel, [(16, 64, 128), (32, 2, 128)], [(2048, 128), (2, 128, 128)]
    )(back)
    gram = lax.all_to_all(gram, ("gx", "gy"), 0, 0)
    (gram,) = call(spread_kernel, [(16, 2, 128)])(gram)
    gram = lax.all_to_all(gram, "gz", 0, 0)
    basis, factor = call(
        finish_kernel,
        [(16, 64, 128), (16, 16)],
        [(16, 16, 128), (16, 64, 128)],
        inputs=2,
        send=16,
    )(gram, image_rows)
    return (basis.reshape(probes.shape), factor)


def solution(mesh):
    in_specs = (
        P("gx", "gy", "gz"),
        P("gx", "gy", "gz"),
        P("gx", "gy", "gz"),
        P(None, "gx", "gy", "gz"),
    )
    out_specs = (P(None, "gx", "gy", "gz"), P())
    return jax.shard_map(
        on_device, mesh=mesh, in_specs=in_specs, out_specs=out_specs, check_vma=False
    )
```

```python
import jax
import jax.numpy as jnp
from jax import lax
from jax.experimental import pallas as pl
from jax.experimental.pallas import tpu as pltpu
from jax.sharding import PartitionSpec as P

DEG = 4
SHIFT = 0.5
LOWER = 0.5
UPPER = 33.5
MID = (UPPER + LOWER) / 2.0
HALF = (UPPER - LOWER) / 2.0
RATIO = MID / HALF

PROBES = 16
CELLS = 32 * 64 * 2048
WIN = 16
HALO = 2 * DEG + 2
INNER = DEG + 1
ROWS = WIN + 2 * HALO
UNROLL = 16
MSG = 12 * HALO + 4 * INNER
F32 = jnp.float32

PATHS = (
    ((0, 0), (0, 1), (1, 1), (1, 2), (0, 2), (0, 3), (1, 3), (1, 0)),
    ((1, 0), (1, 1), (2, 1), (2, 2), (1, 2), (1, 3), (2, 3), (2, 0)),
)


def place(block, w, q):
    core, layer = block % 2, block // 2
    gx = (PATHS[core][w][0] + 2 * (q + layer)) % 8
    return gx, PATHS[core][w][1]


def placer():
    block = lax.axis_index("gz")
    core, layer = block % 2, block // 2

    def number(w, q):
        (x0, y0), (x1, y1) = PATHS[0][w], PATHS[1][w]
        gx = (x0 + core * (x1 - x0) + 2 * (q + layer)) % 8
        return gx * 4 + y0 + core * (y1 - y0)

    return number


def lane_sub():
    lane = lax.broadcasted_iota(jnp.int32, (8, 128), 1)
    return lane, lax.broadcasted_iota(jnp.int32, (8, 128), 0)


def swap_groups(v):
    last = v[0].ndim - 1
    lane = lax.broadcasted_iota(jnp.int32, v[0].shape, last)
    high, low = (lane & 64) == 0, (lane & 32) == 0
    u = [None] * 4
    for a in range(2):
        moved = pltpu.roll(jnp.where(high, v[a + 2], v[a]), 64, last)
        u[a] = jnp.where(high, v[a], moved)
        u[a + 2] = jnp.where(high, moved, v[a + 2])
    out = [None] * 4
    for a in (0, 2):
        out[a] = jnp.where(low, u[a], pltpu.roll(u[a + 1], 32, last))
        out[a + 1] = jnp.where(low, pltpu.roll(u[a], 96, last), u[a + 1])
    return out


def pack_kernel(
    lp_hbm, pr_hbm, dw_hbm, v_hbm, out_ref,
    lp_ref, pr_ref, dw_ref, v_ref, perm_ref, mix_ref, in_sems,
):
    pairs = [(lp_hbm, lp_ref), (pr_hbm, pr_ref), (dw_hbm, dw_ref)]
    pairs += [(v_hbm.at[pl.ds(4 * q, 4)], v_ref.at[pl.ds(4 * q, 4)]) for q in range(4)]
    copies = [pltpu.make_async_copy(a, b, in_sems.at[i]) for i, (a, b) in enumerate(pairs)]
    for copy in copies:
        copy.start()
    first = (lane_sub()[0] & 2) == 0
    number = placer()
    dest = [[number(w, q) for q in range(4)] for w in range(8)]

    def mixed(parts, at):
        for slot in range(4):
            mix_ref[at, pl.ds(slot, 32, stride=4), :] = parts[slot]
        return mix_ref[at].T

    def half(ref, yl):
        return ref[pl.ds(yl, 32, stride=2), :]

    def paired(tile, w):
        return jnp.where(first, tile[16 * w : 16 * w + 8], tile[16 * w + 8 : 16 * w + 16])

    for copy in copies[:3]:
        copy.wait()
    perm_ref[...] = jnp.exp(lp_ref[...])
    perm = [half(perm_ref, yl) for yl in range(2)]
    tiles = [mixed([perm[yl], half(pr_ref, yl)] * 2, yl) for yl in range(2)]
    tiles.append(mixed([half(dw_ref, 0), half(dw_ref, 1)] * 2, 2))
    for w in range(8):
        for i in range(3):
            packed = paired(tiles[i], w)
            for q in range(4):
                out_ref[dest[w][q], 32 + 8 * i : 40 + 8 * i] = packed
    for q in range(4):
        copies[3 + q].wait()
        for yl in range(2):
            fields = [
                perm[yl] * v_ref[4 * q + p, pl.ds(yl, 32, stride=2), :] for p in range(4)
            ]
            tile = mixed(fields, 3 + yl)
            for w in range(8):
                out_ref[dest[w][q], 16 * yl : 16 * yl + 16] = tile[16 * w : 16 * w + 16]


def widen(v, first):
    last = v.ndim - 1
    return jnp.where(first, v, pltpu.roll(v, 2, last)), jnp.where(first, pltpu.roll(v, 126, last), v)


def split(v, even):
    last = v.ndim - 1
    return jnp.where(even, v, pltpu.roll(v, 1, last)), jnp.where(even, pltpu.roll(v, 127, last), v)


def arrange_kernel(in_ref, s_ref, c_ref, w_ref, low_ref, high_ref):
    first = (lane_sub()[0] & 2) == 0

    def fetch(begin, count):
        got = [
            jnp.stack([in_ref[pl.ds(56 * g + begin + k, 8, stride=224), :] for k in range(count)])
            for g in range(4)
        ]
        return swap_groups(got)

    lift, pairs = WIN - HALO, HALO // 2
    for yl in range(2):
        for begin in range(0, WIN, 8):
            for x, v in enumerate(fetch(16 * yl + begin, 8)):
                n = 4 * yl + x
                s_ref[n, begin : begin + 8] = v
                for k in range(8):
                    z = begin + k
                    if z < HALO:
                        low_ref[HALO * n + z] = v[k]
                    if z >= lift:
                        high_ref[HALO * n + z - lift] = v[k]
        for x, v in enumerate(fetch(32 + 8 * yl, 8)):
            n = 4 * yl + x
            below, above = widen(v, first)
            c_ref[n, 0:8] = below
            c_ref[n, 8:16] = above
            c = [below[z] if z < 8 else above[z - 8] for z in range(WIN)]
            for k in range(pairs):
                at = 8 * HALO + pairs * n + k
                low_ref[at] = jnp.where(first, c[k], c[k + pairs])
                high_ref[at] = jnp.where(first, c[lift + k], c[lift + k + pairs])
    for x, v in enumerate(fetch(48, 8)):
        below, above = widen(v, first)
        w_ref[x, 0:8] = below
        w_ref[x, 8:16] = above
        at = 12 * HALO + INNER * x
        low_ref[at : at + INNER] = below[:INNER]
        high_ref[at : at + INNER] = above[8 - INNER :]


FX, FY, FZ, OWN, FAR, COEFS = 0, 8, 16, 24, 32, 38


def far(v):
    return (
        [pltpu.roll(v[n], 7, 1) for n in (0, 4)]
        + [pltpu.roll(v[n], 1, 1) for n in (3, 7)]
        + [pltpu.roll(v[n], 124, 2) for n in range(4)]
        + [pltpu.roll(v[n + 4], 4, 2) for n in range(4)]
    )


def coefficients(perm, press, above, a_ref, b_ref, begin, count):
    lane, sub = lane_sub()
    at, faces = slice(begin, begin + count), slice(begin, begin + above[0][0].shape[0])
    perm_far, press_far = far(perm), far(press)
    none = jnp.zeros((8, 128), F32)
    half = {}
    for n in range(8):
        x_begin = jnp.where(sub == 0, 0.5, 0.0) if n % 4 == 0 else none
        x_end = jnp.where(sub == 7, 0.5, 0.0) if n % 4 == 3 else none
        y_begin = jnp.where(lane < 4, 0.5, 0.0) if n < 4 else none
        y_end = jnp.where(lane >= 124, 0.5, 0.0) if n >= 4 else none
        outside = (x_begin + x_end) + (y_begin + y_end)
        half[n] = (0.5 - x_begin, 0.5 - y_begin)
        for field, field_far, out_ref, sign in (
            (perm, perm_far, a_ref, 1.0),
            (press, press_far, b_ref, -1.0),
        ):
            up = field[n + 1] if n % 4 < 3 else field_far[n // 4]
            out_ref[FX + n, at] = (0.5 - x_end) * (field[n] + sign * up)
            up = field[n + 4] if n < 4 else field_far[n]
            out_ref[FY + n, at] = (0.5 - y_end) * (field[n] + sign * up)
        over_perm, over_press = above[0][n], above[1][n]
        size = over_perm.shape[0]
        a_ref[FZ + n, faces] = 0.5 * (perm[n][:size] + over_perm)
        b_ref[FZ + n, faces] = 0.5 * (press[n][:size] - over_press)
        a_ref[OWN + n, at] = SHIFT + outside * perm[n]
        b_ref[OWN + n, at] = outside * press[n]
    for i, n in enumerate((0, 4, 0, 1, 2, 3)):
        side, k = (half[n][0], 2 + i) if i < 2 else (half[n][1], 6 + i)
        a_ref[FAR + i, at] = side * (perm[n] + perm_far[k])
        b_ref[FAR + i, at] = side * (press_far[k] - press[n])


def sweep(field_ref, begin, end, coef_ref, join, sign, inputs, finish):
    def part(up, down):
        return up - down if sign < 0 else up + down

    def rows(row, count):
        here, below = pl.ds(row, count), pl.ds(row - 1, count + 1)
        now = [field_ref[n, here] for n in range(8)]
        around = far(now)
        flow_x, back_x, flow_y, back_y = ([None] * 8 for _ in range(4))
        for n in range(8):
            up = now[n + 1] if n % 4 < 3 else around[n // 4]
            flow_x[n] = join(now[n], up) * coef_ref[FX + n, here]
            up = now[n + 4] if n < 4 else around[n]
            flow_y[n] = join(now[n], up) * coef_ref[FY + n, here]
        for n in range(8):
            if n % 4:
                back_x[n] = flow_x[n - 1]
            else:
                back_x[n] = join(around[2 + n // 4], now[n]) * coef_ref[FAR + n // 4, here]
            if n >= 4:
                back_y[n] = flow_y[n - 4]
            else:
                back_y[n] = join(around[8 + n], now[n]) * coef_ref[FAR + 2 + n, here]
        results = []
        for n in range(8):
            flow_z = join(field_ref[n, below], field_ref[n, pl.ds(row, count + 1)])
            flow_z = flow_z * coef_ref[FZ + n, below]
            total = coef_ref[OWN + n, here] * now[n] + part(flow_x[n], back_x[n])
            total = total + (part(flow_y[n], back_y[n]) + part(flow_z[1:], flow_z[:-1]))
            extra = [ref[n, here] for ref in inputs]
            results.append((n, finish(row, count, n, now[n], total, *extra)))
        for n, outs in results:
            for ref, value in outs:
                ref[n, here] = value

    steps, rest = divmod(end - begin, UNROLL)

    def body(i, carry):
        rows(begin + UNROLL * i, UNROLL)
        return carry

    lax.fori_loop(0, steps, body, 0)
    if rest:
        rows(end - rest, rest)


def add(a, b):
    return a + b


def minus(a, b):
    return a - b


def step_table():
    table, keep_now, take_now, weight_now = [], 0.0, 1.0 / MID, 1.0 / RATIO
    for _ in range(DEG):
        weight_next = 1.0 / (2.0 * RATIO - weight_now)
        keep, take = weight_next * weight_now, 2.0 * weight_next / HALF
        table.append((keep + take / take_now, take * keep_now / take_now, take))
        keep_now, take_now, weight_now = keep, take, weight_next
    return table


def direction_of(repeat, v, total, old):
    grow, drop, take = step_table()[repeat]
    direction = grow * v - take * total
    return direction - drop * old[0] if repeat else direction


def own_kernel(edge_ref, s_ref, c_ref, w_ref, a_ref, b_ref, perm_ref, wt_ref, e_ref):
    even = (lane_sub()[0] & 1) == 0
    for x in range(4):
        wt_ref[x], wt_ref[4 + x] = split(w_ref[x], even)
    for begin in range(0, WIN, 8):
        parts = [split(c_ref[n, begin : begin + 8], even) for n in range(8)]
        perm, press = [p[0] for p in parts], [p[1] for p in parts]
        more = begin + 8 < WIN
        if more:
            after = [split(c_ref[n, begin + 8 : begin + 9], even) for n in range(8)]
            above = [[jnp.concatenate([v[1:], u[i]]) for v, u in zip((perm, press)[i], after)] for i in range(2)]
        else:
            above = [[v[1:] for v in field] for field in (perm, press)]
        coefficients(perm, press, above, a_ref, b_ref, begin, 8)
        for n in range(8):
            perm_ref[n, begin : begin + 8] = perm[n]
            for row, end in ((0, edge_ref[0]), (WIN - 1, edge_ref[1])):
                if begin <= row < begin + 8:
                    extra = 0.5 * end.astype(F32)
                    a_ref[OWN + n, row] = a_ref[OWN + n, row] + extra * perm[n][row - begin]
                    b_ref[OWN + n, row] = b_ref[OWN + n, row] + extra * press[n][row - begin]

    directions = [e_ref.at[i] for i in range(DEG)]

    def start(row, count, n, v, total):
        return [(directions[0], total * (1.0 / MID))]

    sweep(s_ref, 1, WIN - 1, b_ref, add, -1, (), start)
    for repeat in range(DEG - 1):

        def finish(row, count, n, v, total, *old, i=repeat):
            return [(directions[i + 1], direction_of(i, v, total, old))]

        old = directions[repeat - 1 : repeat] if repeat else ()
        begin = 2 + repeat
        sweep(directions[repeat], begin, WIN - begin, a_ref, minus, -1, old, finish)


def core_kernel(
    edge_ref, lo_ref, s_own_ref, c_own_ref, a_own_ref, b_own_ref, perm_ref, wt_own_ref, e_own_ref, hi_ref,
    out_ref,
    a_ref, b_ref, wt_ref, s_ref, *e_refs,
):
    image_ref = e_refs[1]
    first, even = (lane_sub()[0] & 2) == 0, (lane_sub()[0] & 1) == 0
    top = HALO + WIN

    def halo(src_ref):
        pairs = HALO // 2
        perm, press = [], []
        for n in range(8):
            begin = 8 * HALO + pairs * n
            wide = widen(src_ref[begin : begin + pairs], first)
            both = split(jnp.concatenate(wide), even)
            perm.append(both[0])
            press.append(both[1])
        return perm, press

    def rim(row):
        both = [split(c_own_ref[n, row : row + 1], even) for n in range(8)]
        return [v[0] for v in both], [v[1] for v in both]

    for n in range(8):
        s_ref[n, HALO:top] = s_own_ref[n]
        s_ref[n, :HALO] = lo_ref[HALO * n : HALO * n + HALO]
        s_ref[n, top:] = hi_ref[HALO * n : HALO * n + HALO]
        wt_ref[n, INNER : INNER + WIN] = wt_own_ref[n]
    for src_ref, at in ((lo_ref, slice(0, INNER)), (hi_ref, slice(INNER + WIN, 2 * INNER + WIN))):
        for x in range(4):
            begin = 12 * HALO + INNER * x
            wt_ref[x, at], wt_ref[4 + x, at] = split(src_ref[begin : begin + INNER], even)

    perm, press = halo(lo_ref)
    above = [
        [jnp.concatenate([v[1:], u]) for v, u in zip(field, over)]
        for field, over in zip((perm, press), rim(0))
    ]
    coefficients(perm, press, above, a_ref, b_ref, 0, HALO)
    perm, press = halo(hi_ref)
    here = [
        [jnp.concatenate([u, v[:-1]]) for v, u in zip(field, under)]
        for field, under in zip((perm, press), rim(WIN - 1))
    ]
    coefficients(here[0], here[1], (perm, press), a_ref, b_ref, top - 1, HALO)
    for ref, own_ref in ((a_ref, a_own_ref), (b_ref, b_own_ref)):
        for i in range(COEFS):
            size = WIN - 1 if FZ <= i < OWN else WIN
            ref[i, HALO : HALO + size] = own_ref[i, :size]
        for n in range(8):
            for row, end in ((HALO - 1, 0), (top - 1, 1)):
                ref[FZ + n, row] = ref[FZ + n, row] * (1.0 - edge_ref[end].astype(F32))

    def solve(lowest, finish_last, known):
        for repeat in range(DEG):
            last = repeat == DEG - 1

            def finish(row, count, n, v, total, *old, i=repeat):
                direction = direction_of(i, v, total, old)
                if i < DEG - 1:
                    return [(e_refs[i + 1], direction)]
                iterate = direction + v
                for e in old:
                    iterate = iterate + e
                return finish_last(row, count, n, iterate)

            old = e_refs[repeat - 1 :: -1] if last else e_refs[repeat - 1 : repeat]
            old = old if repeat else ()
            begin = lowest + 1 + repeat
            ranges = [(begin, ROWS - begin)]
            if known and not last:
                ranges = around(begin)
                keep(repeat + 1, begin)
            for low, high in ranges:
                sweep(e_refs[repeat], low, high, a_ref, minus, -1, old, finish)

    def around(begin):
        return [(begin, begin + HALO), (ROWS - begin - HALO, ROWS - begin)]

    def keep(i, begin):
        for n in range(8):
            e_refs[i][n, begin + HALO : ROWS - begin - HALO] = e_own_ref[i, n, begin : WIN - begin]

    def start(row, count, n, v, total):
        return [(e_refs[0], total * (1.0 / MID))]

    keep(0, 1)
    for low, high in around(1):
        sweep(s_ref, low, high, b_ref, add, -1, (), start)
    skip = HALO - INNER

    def second(row, count, n, value):
        return [(e_refs[0], value * (wt_ref[n, pl.ds(row - skip, count)] * (1.0 / MID)))]

    solve(1, second, True)
    solve(skip, lambda row, count, n, value: [(s_ref, value)], False)

    def image(row, count, n, v, total):
        return [(image_ref, perm_ref[n, pl.ds(row - HALO, count)] * total)]

    sweep(s_ref, HALO, top, b_ref, minus, 1, (), image)

    for yl in range(2):
        for begin in range(0, WIN, 8):
            at = slice(HALO + begin, HALO + begin + 8)
            v = swap_groups([image_ref[4 * yl + x, at] for x in range(4)])
            for g in range(4):
                for k in range(8):
                    to = g * 2 * WIN + yl * WIN + begin + k
                    out_ref[pl.ds(to, 8, stride=8 * WIN), :] = v[g][k]


def gram_kernel(in_ref, img_ref, gram_ref, acc_ref, mix_ref):
    number = placer()
    for q in range(4):
        source = [number(w, q) for w in range(8)]
        for yl in range(2):
            rows = [in_ref[source[w], 16 * yl : 16 * yl + 16] for w in range(8)]
            mix_ref[yl] = jnp.concatenate(rows, axis=0).T
            for p in range(4):
                img_ref[4 * q + p, pl.ds(yl, 32, stride=2), :] = mix_ref[
                    yl, pl.ds(p, 32, stride=4), :
                ]
    for i in range(PROBES):
        a = [img_ref[i, 8 * k : 8 * k + 8] for k in range(8)]
        for j in range(i + 1):
            parts = [a[k] * img_ref[j, 8 * k : 8 * k + 8] for k in range(8)]
            while len(parts) > 1:
                parts = [parts[k] + parts[k + 1] for k in range(0, len(parts), 2)]
            begin = (16 * i + j) * 8
            acc_ref[begin : begin + 8] = parts[0]
            begin = (16 * j + i) * 8
            acc_ref[begin : begin + 8] = parts[0]
    sums = []
    for c in range(32):
        parts = [acc_ref[pl.ds(64 * c + s, 8, stride=8), :] for s in range(8)]
        while len(parts) > 1:
            parts = [parts[k] + parts[k + 1] for k in range(0, len(parts), 2)]
        sums.append(parts[0])
    total = lax.dot_general(
        jnp.ones((8, 128), F32),
        jnp.concatenate(sums, axis=0),
        (((1,), (1,)), ((), ())),
        precision=lax.Precision.HIGHEST,
        preferred_element_type=F32,
    )
    _, sub = lane_sub()
    tile = jnp.where(sub == 0, total[:, :128], total[:, 128:])
    for d in range(32):
        gram_ref[d] = tile[0:2]


def spread_kernel(in_ref, out_ref):
    total = jnp.sum(in_ref[...], axis=0)
    for d in range(16):
        out_ref[d] = total


def finish_kernel(gram_ref, img_ref, out_hbm, factor_ref, out_ref, sems):
    total = jnp.sum(gram_ref[...], axis=0) * (1.0 / CELLS)
    lane = lax.broadcasted_iota(jnp.int32, (16, 128), 1)
    row = lax.broadcasted_iota(jnp.int32, (16, 128), 0)
    g = jnp.concatenate(
        [jnp.broadcast_to(total[0:1], (8, 128)), jnp.broadcast_to(total[1:2], (8, 128))], axis=0
    )
    g = jnp.where((lane >> 4) == (row & 7), g, 0.0)
    for step in (16, 32, 64):
        g = g + pltpu.roll(g, step, 1)
    column = [jnp.broadcast_to(g[:, j : j + 1], (16, 128)) for j in range(PROBES)]
    inverse = [jnp.where(row == j, 1.0, 0.0) for j in range(PROBES)]
    factor = jnp.zeros((16, 128), F32)
    for k in range(PROBES):
        pivot = jnp.broadcast_to(column[k][k : k + 1], (16, 128))
        scale = 1.0 / jnp.sqrt(pivot)
        for j in range(k, PROBES):
            factor = jnp.where((lane == j) & (row == k), column[j] * scale, factor)
        value = None
        for j in range(k + 1):
            weight = jnp.broadcast_to(inverse[j][k : k + 1] * scale[:1], (64, 128))
            term = weight * img_ref[j]
            value = term if value is None else value + term
        out_ref[k] = value
        pltpu.make_async_copy(out_ref.at[k], out_hbm.at[k], sems.at[k]).start()
        ratio = jnp.where(row > k, column[k] / pivot, 0.0)
        for j in range(k + 1, PROBES):
            column[j] = column[j] - ratio * jnp.broadcast_to(column[j][k : k + 1], (16, 128))
        for j in range(k + 1):
            inverse[j] = inverse[j] - ratio * jnp.broadcast_to(inverse[j][k : k + 1], (16, 128))
    factor_ref[...] = factor[:, :16]
    for i in range(PROBES):
        pltpu.make_async_copy(out_ref.at[i], out_hbm.at[i], sems.at[i]).wait()


def call(kernel, out_shapes, scratch=(), smem=0, inputs=1, fetch=0, send=0, cost=0):
    out_shape = [jax.ShapeDtypeStruct(s, F32) for s in out_shapes]
    vmem = pl.BlockSpec(memory_space=pltpu.VMEM)
    hbm = pl.BlockSpec(memory_space=pl.ANY)
    specs = [pl.BlockSpec(memory_space=pltpu.SMEM)] * smem + [hbm if fetch else vmem] * inputs
    return pl.pallas_call(
        kernel,
        out_shape=out_shape,
        in_specs=specs,
        out_specs=[hbm if send else vmem] + [vmem] * (len(out_shape) - 1),
        scratch_shapes=[pltpu.VMEM(s, F32) for s in scratch]
        + [pltpu.SemaphoreType.DMA((n,)) for n in (fetch, send) if n],
        compiler_params=pltpu.CompilerParams(vmem_limit_bytes=40 * 1024 * 1024),
        cost_estimate=pl.CostEstimate(flops=cost, bytes_accessed=cost, transcendentals=0) if cost else None,
    )


def on_device(log_perm, pressure, data_weight, probes):
    planes = [a.reshape(64, 128) for a in (log_perm, pressure, data_weight)]
    block = (64, 128)
    scratch = [block, block, block, (16, 64, 128), block, (5, 128, 128)]
    fields = [*planes, probes.reshape(16, 64, 128)]
    (sent,) = call(pack_kernel, [(32, 56, 128)], scratch, inputs=4, fetch=7)(
        *[pltpu.with_memory_space_constraint(a, pltpu.HBM) for a in fields]
    )
    got = lax.all_to_all(sent, ("gx", "gy"), 0, 0)
    plane, msg = (8, WIN, 8, 128), (MSG, 8, 128)
    own_s, own_c, own_w, low, high = call(
        arrange_kernel, [plane, plane, (4, WIN, 8, 128), msg, msg]
    )(got.reshape(32 * 56, 128))

    blocks = lax.axis_size("gz")
    up = []
    for q in range(4):
        route = []
        for n in range(8 * blocks):
            gx, gy = place(n // 8, n % 8, q)
            route.append((gx * 4 + gy) * blocks + n // 8)
        up += [(route[n], route[n + 1]) for n in range(len(route) - 1)]
    down = [(j, i) for i, j in up]
    from_below = lax.ppermute(high, ("gx", "gy", "gz"), up)
    from_above = lax.ppermute(low, ("gx", "gy", "gz"), down)
    block = lax.axis_index("gz")
    at_end = (lax.axis_index("gx") % 2 == 0) & (lax.axis_index("gy") == 0)
    edge = jnp.stack([at_end & (block == 0), at_end & (block == blocks - 1)]).astype(jnp.int32)
    field, plane = (8, ROWS, 8, 128), (8, WIN, 8, 128)
    window, whole = (COEFS, WIN, 8, 128), (COEFS, ROWS, 8, 128)
    a_own, b_own, perm, weight, directions = call(
        own_kernel, [window, window, plane, plane, (DEG,) + plane], smem=1, inputs=3, cost=6_000_000
    )(edge, own_s, own_c, own_w)
    scratch = [whole] * 2 + [(8, WIN + 2 * INNER, 8, 128)] + [field] * 5
    (images,) = call(core_kernel, [(1024, 128)], scratch, smem=1, inputs=9)(
        edge, from_below, own_s, own_c, a_own, b_own, perm, weight, directions, from_above
    )
    back = lax.all_to_all(images.reshape(32, 32, 128), ("gx", "gy"), 0, 0)
    image_rows, gram = call(
        gram_kernel, [(16, 64, 128), (32, 2, 128)], [(2048, 128), (2, 128, 128)]
    )(back)
    gram = lax.all_to_all(gram, ("gx", "gy"), 0, 0)
    (gram,) = call(spread_kernel, [(16, 2, 128)])(gram)
    gram = lax.all_to_all(gram, "gz", 0, 0)
    basis, factor = call(
        finish_kernel,
        [(16, 64, 128), (16, 16)],
        [(16, 64, 128)],
        inputs=2,
        send=16,
    )(gram, image_rows)
    return (basis.reshape(probes.shape), factor)


def solution(mesh):
    in_specs = (
        P("gx", "gy", "gz"),
        P("gx", "gy", "gz"),
        P("gx", "gy", "gz"),
        P(None, "gx", "gy", "gz"),
    )
    out_specs = (P(None, "gx", "gy", "gz"), P())
    return jax.shard_map(
        on_device, mesh=mesh, in_specs=in_specs, out_specs=out_specs, check_vma=False
    )
```

```python
import jax
import jax.numpy as jnp
from jax import lax
from jax.experimental import pallas as pl
from jax.experimental.pallas import tpu as pltpu
from jax.sharding import PartitionSpec as P

DEG = 4
SHIFT = 0.5
LOWER = 0.5
UPPER = 33.5
MID = (UPPER + LOWER) / 2.0
HALF = (UPPER - LOWER) / 2.0
RATIO = MID / HALF

PROBES = 16
CELLS = 32 * 64 * 2048
WIN = 16
HALO = 2 * DEG + 2
INNER = DEG + 1
ROWS = WIN + 2 * HALO
UNROLL = 16
MSG = 12 * HALO + 4 * INNER
F32 = jnp.float32

PATHS = (
    ((0, 0), (0, 1), (1, 1), (1, 2), (0, 2), (0, 3), (1, 3), (1, 0)),
    ((1, 0), (1, 1), (2, 1), (2, 2), (1, 2), (1, 3), (2, 3), (2, 0)),
)


def place(block, w, q):
    core, layer = block % 2, block // 2
    gx = (PATHS[core][w][0] + 2 * (q + layer)) % 8
    return gx, PATHS[core][w][1]


def placer():
    block = lax.axis_index("gz")
    core, layer = block % 2, block // 2

    def number(w, q):
        (x0, y0), (x1, y1) = PATHS[0][w], PATHS[1][w]
        gx = (x0 + core * (x1 - x0) + 2 * (q + layer)) % 8
        return gx * 4 + y0 + core * (y1 - y0)

    return number


def lane_sub():
    lane = lax.broadcasted_iota(jnp.int32, (8, 128), 1)
    return lane, lax.broadcasted_iota(jnp.int32, (8, 128), 0)


def swap_groups(v):
    last = v[0].ndim - 1
    lane = lax.broadcasted_iota(jnp.int32, v[0].shape, last)
    high, low = (lane & 64) == 0, (lane & 32) == 0
    u = [None] * 4
    for a in range(2):
        moved = pltpu.roll(jnp.where(high, v[a + 2], v[a]), 64, last)
        u[a] = jnp.where(high, v[a], moved)
        u[a + 2] = jnp.where(high, moved, v[a + 2])
    out = [None] * 4
    for a in (0, 2):
        out[a] = jnp.where(low, u[a], pltpu.roll(u[a + 1], 32, last))
        out[a + 1] = jnp.where(low, pltpu.roll(u[a], 96, last), u[a + 1])
    return out


def pack_kernel(
    lp_hbm, pr_hbm, dw_hbm, v_hbm, out_ref,
    lp_ref, pr_ref, dw_ref, v_ref, perm_ref, mix_ref, in_sems,
):
    pairs = [(lp_hbm, lp_ref), (pr_hbm, pr_ref), (dw_hbm, dw_ref)]
    pairs += [(v_hbm.at[pl.ds(4 * q, 4)], v_ref.at[pl.ds(4 * q, 4)]) for q in range(4)]
    copies = [pltpu.make_async_copy(a, b, in_sems.at[i]) for i, (a, b) in enumerate(pairs)]
    for copy in copies:
        copy.start()
    first = (lane_sub()[0] & 2) == 0
    number = placer()
    dest = [[number(w, q) for q in range(4)] for w in range(8)]

    def mixed(parts, at):
        for slot in range(4):
            mix_ref[at, pl.ds(slot, 32, stride=4), :] = parts[slot]
        return mix_ref[at].T

    def half(ref, yl):
        return ref[pl.ds(yl, 32, stride=2), :]

    def paired(tile, w):
        return jnp.where(first, tile[16 * w : 16 * w + 8], tile[16 * w + 8 : 16 * w + 16])

    for copy in copies[:3]:
        copy.wait()
    perm_ref[...] = jnp.exp(lp_ref[...])
    perm = [half(perm_ref, yl) for yl in range(2)]
    tiles = [mixed([perm[yl], half(pr_ref, yl)] * 2, yl) for yl in range(2)]
    tiles.append(mixed([half(dw_ref, 0), half(dw_ref, 1)] * 2, 2))
    for w in range(8):
        for i in range(3):
            packed = paired(tiles[i], w)
            for q in range(4):
                out_ref[dest[w][q], 32 + 8 * i : 40 + 8 * i] = packed
    for q in range(4):
        copies[3 + q].wait()
        for yl in range(2):
            fields = [
                perm[yl] * v_ref[4 * q + p, pl.ds(yl, 32, stride=2), :] for p in range(4)
            ]
            tile = mixed(fields, 3 + yl)
            for w in range(8):
                out_ref[dest[w][q], 16 * yl : 16 * yl + 16] = tile[16 * w : 16 * w + 16]


def widen(v, first):
    last = v.ndim - 1
    return jnp.where(first, v, pltpu.roll(v, 2, last)), jnp.where(first, pltpu.roll(v, 126, last), v)


def split(v, even):
    last = v.ndim - 1
    return jnp.where(even, v, pltpu.roll(v, 1, last)), jnp.where(even, pltpu.roll(v, 127, last), v)


def arrange_kernel(in_ref, s_ref, c_ref, w_ref, low_ref, high_ref):
    first = (lane_sub()[0] & 2) == 0

    def fetch(begin, count):
        got = [
            jnp.stack([in_ref[pl.ds(56 * g + begin + k, 8, stride=224), :] for k in range(count)])
            for g in range(4)
        ]
        return swap_groups(got)

    lift, pairs = WIN - HALO, HALO // 2
    for yl in range(2):
        for begin in range(0, WIN, 8):
            for x, v in enumerate(fetch(16 * yl + begin, 8)):
                n = 4 * yl + x
                s_ref[n, begin : begin + 8] = v
                for k in range(8):
                    z = begin + k
                    if z < HALO:
                        low_ref[HALO * n + z] = v[k]
                    if z >= lift:
                        high_ref[HALO * n + z - lift] = v[k]
        for x, v in enumerate(fetch(32 + 8 * yl, 8)):
            n = 4 * yl + x
            below, above = widen(v, first)
            c_ref[n, 0:8] = below
            c_ref[n, 8:16] = above
            c = [below[z] if z < 8 else above[z - 8] for z in range(WIN)]
            for k in range(pairs):
                at = 8 * HALO + pairs * n + k
                low_ref[at] = jnp.where(first, c[k], c[k + pairs])
                high_ref[at] = jnp.where(first, c[lift + k], c[lift + k + pairs])
    for x, v in enumerate(fetch(48, 8)):
        below, above = widen(v, first)
        w_ref[x, 0:8] = below
        w_ref[x, 8:16] = above
        at = 12 * HALO + INNER * x
        low_ref[at : at + INNER] = below[:INNER]
        high_ref[at : at + INNER] = above[8 - INNER :]


FX, FY, FZ, OWN, FAR, COEFS = 0, 8, 16, 24, 32, 38


def far(v):
    return (
        [pltpu.roll(v[n], 7, 1) for n in (0, 4)]
        + [pltpu.roll(v[n], 1, 1) for n in (3, 7)]
        + [pltpu.roll(v[n], 124, 2) for n in range(4)]
        + [pltpu.roll(v[n + 4], 4, 2) for n in range(4)]
    )


def coefficients(perm, press, above, a_ref, b_ref, begin, count):
    lane, sub = lane_sub()
    at, faces = slice(begin, begin + count), slice(begin, begin + above[0][0].shape[0])
    perm_far, press_far = far(perm), far(press)
    none = jnp.zeros((8, 128), F32)
    half = {}
    for n in range(8):
        x_begin = jnp.where(sub == 0, 0.5, 0.0) if n % 4 == 0 else none
        x_end = jnp.where(sub == 7, 0.5, 0.0) if n % 4 == 3 else none
        y_begin = jnp.where(lane < 4, 0.5, 0.0) if n < 4 else none
        y_end = jnp.where(lane >= 124, 0.5, 0.0) if n >= 4 else none
        outside = (x_begin + x_end) + (y_begin + y_end)
        half[n] = (0.5 - x_begin, 0.5 - y_begin)
        for field, field_far, out_ref, sign in (
            (perm, perm_far, a_ref, 1.0),
            (press, press_far, b_ref, -1.0),
        ):
            up = field[n + 1] if n % 4 < 3 else field_far[n // 4]
            out_ref[FX + n, at] = (0.5 - x_end) * (field[n] + sign * up)
            up = field[n + 4] if n < 4 else field_far[n]
            out_ref[FY + n, at] = (0.5 - y_end) * (field[n] + sign * up)
        over_perm, over_press = above[0][n], above[1][n]
        size = over_perm.shape[0]
        a_ref[FZ + n, faces] = 0.5 * (perm[n][:size] + over_perm)
        b_ref[FZ + n, faces] = 0.5 * (press[n][:size] - over_press)
        a_ref[OWN + n, at] = SHIFT + outside * perm[n]
        b_ref[OWN + n, at] = outside * press[n]
    for i, n in enumerate((0, 4, 0, 1, 2, 3)):
        side, k = (half[n][0], 2 + i) if i < 2 else (half[n][1], 6 + i)
        a_ref[FAR + i, at] = side * (perm[n] + perm_far[k])
        b_ref[FAR + i, at] = side * (press_far[k] - press[n])


def sweep(field_ref, begin, end, coef_ref, join, sign, inputs, finish):
    def part(up, down):
        return up - down if sign < 0 else up + down

    def rows(row, count):
        here, below = pl.ds(row, count), pl.ds(row - 1, count + 1)
        now = [field_ref[n, here] for n in range(8)]
        around = far(now)
        flow_x, back_x, flow_y, back_y = ([None] * 8 for _ in range(4))
        for n in range(8):
            up = now[n + 1] if n % 4 < 3 else around[n // 4]
            flow_x[n] = join(now[n], up) * coef_ref[FX + n, here]
            up = now[n + 4] if n < 4 else around[n]
            flow_y[n] = join(now[n], up) * coef_ref[FY + n, here]
        for n in range(8):
            if n % 4:
                back_x[n] = flow_x[n - 1]
            else:
                back_x[n] = join(around[2 + n // 4], now[n]) * coef_ref[FAR + n // 4, here]
            if n >= 4:
                back_y[n] = flow_y[n - 4]
            else:
                back_y[n] = join(around[8 + n], now[n]) * coef_ref[FAR + 2 + n, here]
        results = []
        for n in range(8):
            flow_z = join(field_ref[n, below], field_ref[n, pl.ds(row, count + 1)])
            flow_z = flow_z * coef_ref[FZ + n, below]
            total = coef_ref[OWN + n, here] * now[n] + part(flow_x[n], back_x[n])
            total = total + (part(flow_y[n], back_y[n]) + part(flow_z[1:], flow_z[:-1]))
            extra = [ref[n, here] for ref in inputs]
            results.append((n, finish(row, count, n, now[n], total, *extra)))
        for n, outs in results:
            for ref, value in outs:
                ref[n, here] = value

    steps, rest = divmod(end - begin, UNROLL)

    def body(i, carry):
        rows(begin + UNROLL * i, UNROLL)
        return carry

    lax.fori_loop(0, steps, body, 0)
    if rest:
        rows(end - rest, rest)


def add(a, b):
    return a + b


def minus(a, b):
    return a - b


def step_table():
    table, keep_now, take_now, weight_now = [], 0.0, 1.0 / MID, 1.0 / RATIO
    for _ in range(DEG):
        weight_next = 1.0 / (2.0 * RATIO - weight_now)
        keep, take = weight_next * weight_now, 2.0 * weight_next / HALF
        table.append((keep + take / take_now, take * keep_now / take_now, take))
        keep_now, take_now, weight_now = keep, take, weight_next
    return table


def direction_of(repeat, v, total, old):
    grow, drop, take = step_table()[repeat]
    direction = grow * v - take * total
    return direction - drop * old[0] if repeat else direction


def own_kernel(edge_ref, s_ref, c_ref, w_ref, a_ref, b_ref, perm_ref, wt_ref, e_ref):
    even = (lane_sub()[0] & 1) == 0
    for x in range(4):
        wt_ref[x], wt_ref[4 + x] = split(w_ref[x], even)
    for begin in range(0, WIN, 8):
        parts = [split(c_ref[n, begin : begin + 8], even) for n in range(8)]
        perm, press = [p[0] for p in parts], [p[1] for p in parts]
        more = begin + 8 < WIN
        if more:
            after = [split(c_ref[n, begin + 8 : begin + 9], even) for n in range(8)]
            above = [[jnp.concatenate([v[1:], u[i]]) for v, u in zip((perm, press)[i], after)] for i in range(2)]
        else:
            above = [[v[1:] for v in field] for field in (perm, press)]
        coefficients(perm, press, above, a_ref, b_ref, begin, 8)
        for n in range(8):
            perm_ref[n, begin : begin + 8] = perm[n]
            for row, end in ((0, edge_ref[0]), (WIN - 1, edge_ref[1])):
                if begin <= row < begin + 8:
                    extra = 0.5 * end.astype(F32)
                    a_ref[OWN + n, row] = a_ref[OWN + n, row] + extra * perm[n][row - begin]
                    b_ref[OWN + n, row] = b_ref[OWN + n, row] + extra * press[n][row - begin]

    directions = [e_ref.at[i] for i in range(DEG)]

    def start(row, count, n, v, total):
        return [(directions[0], total * (1.0 / MID))]

    sweep(s_ref, 1, WIN - 1, b_ref, add, -1, (), start)
    for repeat in range(DEG - 1):

        def finish(row, count, n, v, total, *old, i=repeat):
            return [(directions[i + 1], direction_of(i, v, total, old))]

        old = directions[repeat - 1 : repeat] if repeat else ()
        begin = 2 + repeat
        sweep(directions[repeat], begin, WIN - begin, a_ref, minus, -1, old, finish)


def core_kernel(
    edge_ref, lo_ref, s_own_ref, c_own_ref, a_own_ref, b_own_ref, perm_ref, wt_own_ref, e_own_ref, hi_ref,
    out_ref,
    a_ref, b_ref, wt_ref, s_ref, *e_refs,
):
    image_ref = e_refs[1]
    first, even = (lane_sub()[0] & 2) == 0, (lane_sub()[0] & 1) == 0
    top = HALO + WIN

    def halo(src_ref):
        pairs = HALO // 2
        perm, press = [], []
        for n in range(8):
            begin = 8 * HALO + pairs * n
            wide = widen(src_ref[begin : begin + pairs], first)
            both = split(jnp.concatenate(wide), even)
            perm.append(both[0])
            press.append(both[1])
        return perm, press

    def rim(row):
        both = [split(c_own_ref[n, row : row + 1], even) for n in range(8)]
        return [v[0] for v in both], [v[1] for v in both]

    for n in range(8):
        s_ref[n, HALO:top] = s_own_ref[n]
        s_ref[n, :HALO] = lo_ref[HALO * n : HALO * n + HALO]
        s_ref[n, top:] = hi_ref[HALO * n : HALO * n + HALO]
        wt_ref[n, INNER : INNER + WIN] = wt_own_ref[n]
    for src_ref, at in ((lo_ref, slice(0, INNER)), (hi_ref, slice(INNER + WIN, 2 * INNER + WIN))):
        for x in range(4):
            begin = 12 * HALO + INNER * x
            wt_ref[x, at], wt_ref[4 + x, at] = split(src_ref[begin : begin + INNER], even)

    perm, press = halo(lo_ref)
    above = [
        [jnp.concatenate([v[1:], u]) for v, u in zip(field, over)]
        for field, over in zip((perm, press), rim(0))
    ]
    coefficients(perm, press, above, a_ref, b_ref, 0, HALO)
    perm, press = halo(hi_ref)
    here = [
        [jnp.concatenate([u, v[:-1]]) for v, u in zip(field, under)]
        for field, under in zip((perm, press), rim(WIN - 1))
    ]
    coefficients(here[0], here[1], (perm, press), a_ref, b_ref, top - 1, HALO)
    for ref, own_ref in ((a_ref, a_own_ref), (b_ref, b_own_ref)):
        for i in range(COEFS):
            size = WIN - 1 if FZ <= i < OWN else WIN
            ref[i, HALO : HALO + size] = own_ref[i, :size]
        for n in range(8):
            for row, end in ((HALO - 1, 0), (top - 1, 1)):
                ref[FZ + n, row] = ref[FZ + n, row] * (1.0 - edge_ref[end].astype(F32))

    def solve(lowest, finish_last, known):
        for repeat in range(DEG):
            last = repeat == DEG - 1

            def finish(row, count, n, v, total, *old, i=repeat):
                direction = direction_of(i, v, total, old)
                if i < DEG - 1:
                    return [(e_refs[i + 1], direction)]
                iterate = direction + v
                for e in old:
                    iterate = iterate + e
                return finish_last(row, count, n, iterate)

            old = e_refs[repeat - 1 :: -1] if last else e_refs[repeat - 1 : repeat]
            old = old if repeat else ()
            begin = lowest + 1 + repeat
            ranges = [(begin, ROWS - begin)]
            if known and not last:
                ranges = around(begin)
                keep(repeat + 1, begin)
            for low, high in ranges:
                sweep(e_refs[repeat], low, high, a_ref, minus, -1, old, finish)

    def around(begin):
        return [(begin, begin + HALO), (ROWS - begin - HALO, ROWS - begin)]

    def keep(i, begin):
        for n in range(8):
            e_refs[i][n, begin + HALO : ROWS - begin - HALO] = e_own_ref[i, n, begin : WIN - begin]

    def start(row, count, n, v, total):
        return [(e_refs[0], total * (1.0 / MID))]

    keep(0, 1)
    for low, high in around(1):
        sweep(s_ref, low, high, b_ref, add, -1, (), start)
    skip = HALO - INNER

    def second(row, count, n, value):
        return [(e_refs[0], value * (wt_ref[n, pl.ds(row - skip, count)] * (1.0 / MID)))]

    solve(1, second, True)
    solve(skip, lambda row, count, n, value: [(s_ref, value)], False)

    def image(row, count, n, v, total):
        return [(image_ref, perm_ref[n, pl.ds(row - HALO, count)] * total)]

    sweep(s_ref, HALO, top, b_ref, minus, 1, (), image)

    for yl in range(2):
        for begin in range(0, WIN, 8):
            at = slice(HALO + begin, HALO + begin + 8)
            v = swap_groups([image_ref[4 * yl + x, at] for x in range(4)])
            for g in range(4):
                for k in range(8):
                    to = g * 2 * WIN + yl * WIN + begin + k
                    out_ref[pl.ds(to, 8, stride=8 * WIN), :] = v[g][k]


def gram_kernel(in_ref, img_ref, gram_ref, acc_ref, mix_ref):
    number = placer()
    for q in range(4):
        source = [number(w, q) for w in range(8)]
        for yl in range(2):
            rows = [in_ref[source[w], 16 * yl : 16 * yl + 16] for w in range(8)]
            mix_ref[yl] = jnp.concatenate(rows, axis=0).T
            for p in range(4):
                img_ref[4 * q + p, pl.ds(yl, 32, stride=2), :] = mix_ref[
                    yl, pl.ds(p, 32, stride=4), :
                ]
    for i in range(PROBES):
        a = [img_ref[i, 8 * k : 8 * k + 8] for k in range(8)]
        for j in range(i + 1):
            parts = [a[k] * img_ref[j, 8 * k : 8 * k + 8] for k in range(8)]
            while len(parts) > 1:
                parts = [parts[k] + parts[k + 1] for k in range(0, len(parts), 2)]
            begin = (16 * i + j) * 8
            acc_ref[begin : begin + 8] = parts[0]
            begin = (16 * j + i) * 8
            acc_ref[begin : begin + 8] = parts[0]
    sums = []
    for c in range(32):
        parts = [acc_ref[pl.ds(64 * c + s, 8, stride=8), :] for s in range(8)]
        while len(parts) > 1:
            parts = [parts[k] + parts[k + 1] for k in range(0, len(parts), 2)]
        sums.append(parts[0])
    total = lax.dot_general(
        jnp.ones((8, 128), F32),
        jnp.concatenate(sums, axis=0),
        (((1,), (1,)), ((), ())),
        precision=lax.Precision.HIGHEST,
        preferred_element_type=F32,
    )
    _, sub = lane_sub()
    tile = jnp.where(sub == 0, total[:, :128], total[:, 128:])
    for d in range(16):
        gram_ref[d] = tile[0:2]


def spread_kernel(in_ref, out_ref):
    total = jnp.sum(in_ref[...], axis=0)
    for d in range(32):
        out_ref[d] = total


def finish_kernel(gram_ref, img_ref, out_hbm, factor_ref, out_ref, sems):
    total = jnp.sum(gram_ref[...], axis=0) * (1.0 / CELLS)
    lane = lax.broadcasted_iota(jnp.int32, (16, 128), 1)
    row = lax.broadcasted_iota(jnp.int32, (16, 128), 0)
    g = jnp.concatenate(
        [jnp.broadcast_to(total[0:1], (8, 128)), jnp.broadcast_to(total[1:2], (8, 128))], axis=0
    )
    g = jnp.where((lane >> 4) == (row & 7), g, 0.0)
    for step in (16, 32, 64):
        g = g + pltpu.roll(g, step, 1)
    column = [jnp.broadcast_to(g[:, j : j + 1], (16, 128)) for j in range(PROBES)]
    inverse = [jnp.where(row == j, 1.0, 0.0) for j in range(PROBES)]
    factor = jnp.zeros((16, 128), F32)
    for k in range(PROBES):
        pivot = jnp.broadcast_to(column[k][k : k + 1], (16, 128))
        scale = 1.0 / jnp.sqrt(pivot)
        for j in range(k, PROBES):
            factor = jnp.where((lane == j) & (row == k), column[j] * scale, factor)
        value = None
        for j in range(k + 1):
            weight = jnp.broadcast_to(inverse[j][k : k + 1] * scale[:1], (64, 128))
            term = weight * img_ref[j]
            value = term if value is None else value + term
        out_ref[k] = value
        pltpu.make_async_copy(out_ref.at[k], out_hbm.at[k], sems.at[k]).start()
        ratio = jnp.where(row > k, column[k] / pivot, 0.0)
        for j in range(k + 1, PROBES):
            column[j] = column[j] - ratio * jnp.broadcast_to(column[j][k : k + 1], (16, 128))
        for j in range(k + 1):
            inverse[j] = inverse[j] - ratio * jnp.broadcast_to(inverse[j][k : k + 1], (16, 128))
    factor_ref[...] = factor[:, :16]
    for i in range(PROBES):
        pltpu.make_async_copy(out_ref.at[i], out_hbm.at[i], sems.at[i]).wait()


def call(kernel, out_shapes, scratch=(), smem=0, inputs=1, fetch=0, send=0, cost=0):
    out_shape = [jax.ShapeDtypeStruct(s, F32) for s in out_shapes]
    vmem = pl.BlockSpec(memory_space=pltpu.VMEM)
    hbm = pl.BlockSpec(memory_space=pl.ANY)
    specs = [pl.BlockSpec(memory_space=pltpu.SMEM)] * smem + [hbm if fetch else vmem] * inputs
    return pl.pallas_call(
        kernel,
        out_shape=out_shape,
        in_specs=specs,
        out_specs=[hbm if send else vmem] + [vmem] * (len(out_shape) - 1),
        scratch_shapes=[pltpu.VMEM(s, F32) for s in scratch]
        + [pltpu.SemaphoreType.DMA((n,)) for n in (fetch, send) if n],
        compiler_params=pltpu.CompilerParams(vmem_limit_bytes=40 * 1024 * 1024),
        cost_estimate=pl.CostEstimate(flops=cost, bytes_accessed=cost, transcendentals=0) if cost else None,
    )


def on_device(log_perm, pressure, data_weight, probes):
    planes = [a.reshape(64, 128) for a in (log_perm, pressure, data_weight)]
    block = (64, 128)
    scratch = [block, block, block, (16, 64, 128), block, (5, 128, 128)]
    fields = [*planes, probes.reshape(16, 64, 128)]
    (sent,) = call(pack_kernel, [(32, 56, 128)], scratch, inputs=4, fetch=7)(
        *[pltpu.with_memory_space_constraint(a, pltpu.HBM) for a in fields]
    )
    got = lax.all_to_all(sent, ("gx", "gy"), 0, 0)
    plane, msg = (8, WIN, 8, 128), (MSG, 8, 128)
    own_s, own_c, own_w, low, high = call(
        arrange_kernel, [plane, plane, (4, WIN, 8, 128), msg, msg]
    )(got.reshape(32 * 56, 128))

    blocks = lax.axis_size("gz")
    up = []
    for q in range(4):
        route = []
        for n in range(8 * blocks):
            gx, gy = place(n // 8, n % 8, q)
            route.append((gx * 4 + gy) * blocks + n // 8)
        up += [(route[n], route[n + 1]) for n in range(len(route) - 1)]
    down = [(j, i) for i, j in up]
    from_below = lax.ppermute(high, ("gx", "gy", "gz"), up)
    from_above = lax.ppermute(low, ("gx", "gy", "gz"), down)
    block = lax.axis_index("gz")
    at_end = (lax.axis_index("gx") % 2 == 0) & (lax.axis_index("gy") == 0)
    edge = jnp.stack([at_end & (block == 0), at_end & (block == blocks - 1)]).astype(jnp.int32)
    field, plane = (8, ROWS, 8, 128), (8, WIN, 8, 128)
    window, whole = (COEFS, WIN, 8, 128), (COEFS, ROWS, 8, 128)
    a_own, b_own, perm, weight, directions = call(
        own_kernel, [window, window, plane, plane, (DEG,) + plane], smem=1, inputs=3, cost=6_000_000
    )(edge, own_s, own_c, own_w)
    scratch = [whole] * 2 + [(8, WIN + 2 * INNER, 8, 128)] + [field] * 5
    (images,) = call(core_kernel, [(1024, 128)], scratch, smem=1, inputs=9)(
        edge, from_below, own_s, own_c, a_own, b_own, perm, weight, directions, from_above
    )
    back = lax.all_to_all(images.reshape(32, 32, 128), ("gx", "gy"), 0, 0)
    image_rows, gram = call(
        gram_kernel, [(16, 64, 128), (16, 2, 128)], [(2048, 128), (2, 128, 128)]
    )(back)
    gram = lax.all_to_all(gram, "gz", 0, 0)
    (gram,) = call(spread_kernel, [(32, 2, 128)])(gram)
    gram = lax.all_to_all(gram, ("gx", "gy"), 0, 0)
    basis, factor = call(
        finish_kernel,
        [(16, 64, 128), (16, 16)],
        [(16, 64, 128)],
        inputs=2,
        send=16,
    )(gram, image_rows)
    return (basis.reshape(probes.shape), factor)


def solution(mesh):
    in_specs = (
        P("gx", "gy", "gz"),
        P("gx", "gy", "gz"),
        P("gx", "gy", "gz"),
        P(None, "gx", "gy", "gz"),
    )
    out_specs = (P(None, "gx", "gy", "gz"), P())
    return jax.shard_map(
        on_device, mesh=mesh, in_specs=in_specs, out_specs=out_specs, check_vma=False
    )
```
